512 devices in a mesh: seq: 32 (over z, x_hi, core), tensor: 16 (over y, x_lo).
Axes of the slice: x: 4 (x_hi: 2, x_lo: 2; x = x_hi * 2 + x_lo), y: 8, z: 8, core: 2. Of those that a mesh axis runs over, the one named last changes fastest.
Arguments:
- query: bfloat16 [8192, 4096], P('seq', 'tensor'), may hold values from -6 to 6
- key_branch: bfloat16 [8192, 4096], P('seq', 'tensor'), may hold values from -6 to 6
- value: bfloat16 [8192, 4096], P('seq', 'tensor'), may hold values from -6 to 6
- filters: float32 [256, 8192], P('tensor', 'seq'), may hold values from -4 to 4
- skip: float32 [4096], P('tensor'), may hold values from -4 to 4
- weight: bfloat16 [4096, 8192], P('tensor'), may hold values from -0.09375 to 0.09375
Outputs:
- layer_out: bfloat16 [8192, 8192], P(('seq', 'tensor'))
The draws below stay inside these ranges and needn't reach their ends.
All inputs are finite; a program needn't handle non-finite values.
Results may differ from the reference program's by a relative error of at most 0.029.
Values may be sent and summed in bfloat16 or wider, within the bound.
A program may use at most 64 MiB of HBM per device.

```python
import math
import jax
import jax.numpy as jnp
from jax import lax

C = 4096
D = 8192
GROUP = 16
TOKENS = 8192
CD = 256
GROUPS = 256
N_TENSOR = 16


def draw_filters(key, part):
    key = jax.random.fold_in(key, 7)
    rate_key, noise_key = jax.random.split(key)
    rates = jnp.exp(jax.random.uniform(rate_key, (GROUPS, 1), jnp.float32, math.log(0.5), math.log(40.0)))
    noise = jnp.clip(jax.random.normal(noise_key, (GROUPS, TOKENS), jnp.float32), -4.0, 4.0)
    steps = jnp.arange(TOKENS, dtype=jnp.float32)[None, :] / TOKENS
    decay = jnp.exp(-2.0 * rates * steps) * (2.0 * rates / (1.0 - jnp.exp(-2.0 * rates)))
    envelope = jnp.sqrt((0.7 * decay + 0.3) / TOKENS)
    return (noise * envelope).astype(jnp.float32)


def block_levels(own_key, shape, cuts, low, top_value):
    factor_of, own = 1.0, jax.random.fold_in(own_key, 6)
    for dim, shards_of in cuts:
        draws = jnp.exp(jax.random.uniform(jax.random.fold_in(own, dim), (shards_of,), jnp.float32, low / len(cuts), top_value / len(cuts)))
        factor_of = factor_of * jnp.repeat(draws, shape[dim] // shards_of).reshape([-1 if axis == dim else 1 for axis in range(len(shape))])
    return factor_of


def centred(stream_key, shape, spread, reach, cuts=(), kind=jnp.bfloat16):
    entries = spread * jax.random.normal(stream_key, shape, jnp.float32)
    if cuts:
        entries = entries * block_levels(stream_key, shape, cuts, -0.22, 0.18)
    return jnp.clip(entries, -reach, reach).astype(kind)


def setup_inputs(seed: int = 0) -> dict:
    seeds = jax.random.split(jax.random.key(seed), 7)
    query = centred(seeds[0], (TOKENS, C), 1.0, 6.0, ((0, 32), (1, 16)))
    key_branch = centred(seeds[1], (TOKENS, C), 1.0, 6.0, ((0, 32), (1, 16)))
    value = centred(seeds[2], (TOKENS, C), 1.0, 6.0, ((0, 32), (1, 16)))
    filters = draw_filters(jax.random.fold_in(seeds[6], 71), 0)
    skip = centred(seeds[4], (C,), 1.0, 4.0, ((0, 16),), jnp.float32)
    weight = centred(seeds[5], (C, D), C ** -0.5, 0.09375, ((0, 16),))
    return dict(query=query, key_branch=key_branch, value=value, filters=filters, skip=skip, weight=weight)


def reference(query, key_branch, value, filters, skip, weight):
    mixed = key_branch.astype(jnp.float32) * value.astype(jnp.float32)
    by_group = jnp.transpose(mixed.reshape(TOKENS, GROUPS, GROUP), (1, 0, 2))

    def convolve(pair):
        block, taps = pair
        spectrum = jnp.fft.fft(block, n=2 * TOKENS, axis=0) * jnp.fft.fft(taps, n=2 * TOKENS)[:, None]
        return jnp.real(jnp.fft.ifft(spectrum, axis=0))[:TOKENS].astype(jnp.float32)

    response = lax.map(convolve, (by_group, filters))
    response = jnp.transpose(response, (1, 0, 2)).reshape(TOKENS, C)
    gated = (query.astype(jnp.float32) * (response + skip[None, :] * mixed)).astype(jnp.bfloat16)
    blocks = jnp.transpose(gated.reshape(TOKENS, N_TENSOR, CD), (1, 0, 2))
    weight_blocks = weight.reshape(N_TENSOR, CD, D)

    def add_block(total, pair):
        piece, block_weight = pair
        term = jnp.dot(piece, block_weight, preferred_element_type=jnp.float32).astype(jnp.bfloat16)
        term = lax.optimization_barrier(term)
        return total + term.astype(jnp.float32), None

    projected, _ = lax.scan(add_block, jnp.zeros((TOKENS, D), jnp.float32), (blocks, weight_blocks))
    return projected.astype(jnp.bfloat16)
```

```python
import functools

import jax
import jax.numpy as jnp
from jax import lax
from jax.experimental import pallas as pl
from jax.experimental.pallas import tpu as pltpu
from jax.sharding import PartitionSpec as P

F32 = jnp.float32
BF16 = jnp.bfloat16
LANES = 128
SLAB = 8
BLOCK = 2 * LANES
UNROLL = 4
CHUNKS = 8


def remote(src, dst, send, recv, device):
    return pltpu.make_async_remote_copy(
        src_ref=src,
        dst_ref=dst,
        send_sem=send,
        recv_sem=recv,
        device_id=device,
        device_id_type=pl.DeviceIdType.MESH,
    )


def kernel(
    S, Y,
    query, key, value, filters, skip, weight, out,
    sx, rx, sf, rf, toeplitz, lhs, acc, sy, ry, gated, gated_x, wv, part, ss, sr, fo,
    x_send, x_recv, f_send, f_recv, y_send, y_recv, w_local, wd_send, wd_recv, wf_send, wf_recv,
    g_sem, r_send, r_recv, o_send, o_recv,
):
    seq = lax.axis_index("seq")
    ten = lax.axis_index("tensor")
    y = ten // 2
    xl = ten % 2
    core = seq % 2
    across = (seq, ten + 1 - 2 * xl)
    beside = (seq + 1 - 2 * core, ten)
    ahead = (seq, (ten + 2) % (2 * Y))
    behind = (seq, (ten + 2 * Y - 2) % (2 * Y))
    width = query.shape[1]
    columns = weight.shape[1]
    wide = columns // 2
    chunk = wide // CHUNKS
    half = CHUNKS // 2
    rows = BLOCK // Y

    barrier = pltpu.get_barrier_semaphore()

    def greet(device):
        pl.semaphore_signal(barrier, inc=1, device_id=device, device_id_type=pl.DeviceIdType.MESH)

    for device in (across, ahead, behind):
        greet(device)

    def greet_seq(d, _):
        greet(((seq + d) % S, ten))
        return 0

    lax.fori_loop(1, S, greet_seq, 0)

    def own_weight(j):
        return pltpu.make_async_copy(
            weight.at[:, pl.ds(pl.multiple_of(xl * wide + j * chunk, LANES), chunk)], wv.at[0, j], w_local.at[j]
        )

    for j in range(CHUNKS):
        own_weight(j).start()

    mixed = key[...].astype(F32) * value[...].astype(F32)
    turned = mixed.T
    sx[...] = jnp.concatenate(
        [turned[:, :LANES].reshape(S, SLAB, LANES), turned[:, LANES:].reshape(S, SLAB, LANES)], axis=1
    ).astype(BF16)
    for g in range(filters.shape[0]):
        for h in range(2):
            sf[g, h : h + 1, :] = filters[g : g + 1, h * LANES : (h + 1) * LANES]
    rx[pl.ds(seq, 1)] = sx[pl.ds(seq, 1)]
    rf[pl.ds(seq, 1)] = sf[pl.ds(seq // 2, 1)]

    pl.semaphore_wait(barrier, S + 2)

    def taps_copy(d):
        p = (seq + d) % S
        return remote(sf.at[p // 2], rf.at[seq], f_send.at[d], f_recv.at[d], (p, ten))

    def taps_wait(d):
        s = (seq + S - d) % S
        remote(sf.at[0], rf.at[s], f_send.at[d], f_recv.at[d], (s, ten)).wait_recv()

    def signal_copy(d):
        p = (seq + d) % S
        return remote(sx.at[p], rx.at[seq], x_send.at[d], x_recv.at[d], (p, ten))

    def signal_wait(d):
        s = (seq + S - d) % S
        remote(sx.at[s], rx.at[s], x_send.at[d], x_recv.at[d], (s, ten)).wait_recv()

    def response_copy(d):
        p = (seq + d) % S
        return remote(sy.at[p], ry.at[seq], y_send.at[d], y_recv.at[d], (p, ten))

    def response_wait(d):
        s = (seq + S - d) % S
        remote(sy.at[s], ry.at[s], y_send.at[d], y_recv.at[d], (s, ten)).wait_recv()

    def each(function):
        def step(d, _):
            function(d)
            return 0

        lax.fori_loop(1, S, step, 0)

    each(lambda d: taps_copy(d).start())
    each(lambda d: signal_copy(d).start())

    def direct(i):
        j = core * half + i
        return remote(
            weight.at[:, pl.ds(pl.multiple_of((1 - xl) * wide + j * chunk, LANES), chunk)],
            wv.at[1, j], wd_send.at[i], wd_recv.at[i], across,
        )

    def forward(i):
        j = core * half + i
        return remote(wv.at[1, j], wv.at[1, j], wf_send.at[i], wf_recv.at[i], beside)

    def forwarded(i):
        j = (1 - core) * half + i
        return remote(wv.at[1, j], wv.at[1, j], wf_send.at[i], wf_recv.at[i], beside)

    for i in range(half):
        direct(i).start()

    each(taps_wait)
    toeplitz[0, 1, :, 0:LANES] = jnp.zeros((LANES, LANES), BF16)
    lane = lax.broadcasted_iota(jnp.int32, (LANES, LANES), 1)
    down = lax.broadcasted_iota(jnp.int32, (LANES, LANES), 0)
    mask = lane >= down

    def build(a, before):
        for h in range(2):
            row = jnp.broadcast_to(rf[a, h : h + 1, :], (LANES, LANES))
            rolled = pltpu.roll(row, 0, 1, stride=1, stride_axis=0)
            block = jnp.where(mask, rolled, before).astype(BF16)
            before = rolled
            if h == 0:
                toeplitz[a, 0, :, 0:LANES] = block
                toeplitz[a, 1, :, LANES:BLOCK] = block
            else:
                toeplitz[a, 0, :, LANES:BLOCK] = block
                toeplitz[a + 1, 1, :, 0:LANES] = block
        return before

    lax.fori_loop(0, S, build, jnp.zeros((LANES, LANES), F32))

    each(signal_wait)
    signal = rx[...].astype(F32)
    for h in range(2):
        piece = signal[:, h * SLAB : (h + 1) * SLAB, :].reshape(S * SLAB, LANES)
        for r in range(UNROLL):
            shifted = piece
            if r > 0:
                shifted = jnp.concatenate([jnp.zeros((r * SLAB, LANES), F32), piece[: (S - r) * SLAB]], axis=0)
            lhs[:, r * BLOCK + h * LANES : r * BLOCK + (h + 1) * LANES] = shifted.astype(BF16)
    for step in range(S // UNROLL):
        top = step * UNROLL * SLAB
        taps = toeplitz[step * UNROLL : (step + 1) * UNROLL].reshape(UNROLL * BLOCK, BLOCK)
        product = jnp.dot(lhs[: S * SLAB - top, :], taps, preferred_element_type=F32)
        if step == 0:
            acc[...] = product
        else:
            acc[top:, :] += product
    sy[...] = jnp.concatenate(
        [acc[:, :LANES].reshape(S, SLAB, LANES), acc[:, LANES:].reshape(S, SLAB, LANES)], axis=1
    ).astype(BF16)
    each(lambda d: response_copy(d).start())
    ry[pl.ds(seq, 1)] = sy[pl.ds(seq, 1)]

    for i in range(half):
        direct(i).wait_recv()
        forward(i).start()

    each(response_wait)
    answer = ry[...].astype(F32)
    for h in range(2):
        span = slice(h * LANES, (h + 1) * LANES)
        response = answer[:, h * SLAB : (h + 1) * SLAB, :].reshape(width, LANES).T
        signal = key[span, :].astype(F32) * value[span, :].astype(F32)
        gated[span, :] = (query[span, :].astype(F32) * (response + skip[...] * signal)).astype(BF16)

    exchange = remote(gated, gated_x, g_sem.at[0], g_sem.at[1], across)
    exchange.start()
    for j in range(CHUNKS):
        own_weight(j).wait()
    exchange.wait_recv()

    steps = [((Y - 1) // 2, Y // 2), (Y // 2, (Y - 1) // 2)]

    def hop(i, slot, device):
        return remote(ss.at[i, slot], sr.at[i, slot], r_send.at[i, slot], r_recv.at[i, slot], device)

    def pairs(function):
        def step(pair, _):
            for parity in range(2):
                function(2 * pair + parity, *steps[parity])
            return 0

        lax.fori_loop(0, half, step, 0)

    def project(i, up, low):
        j = (core * half + i) % CHUNKS
        term = jnp.dot(gated[...], wv[0, j], preferred_element_type=F32)
        term = term + jnp.dot(gated_x[...], wv[1, j], preferred_element_type=F32)
        part[i] = term.reshape(Y, rows, chunk)
        advance(0, i, up, low)

    def advance(s, i, up, low):
        for slot, count, device, owner in (
            (0, up, ahead, (y + up - s) % Y),
            (up, low, behind, (y + Y - low + s) % Y),
        ):
            if s >= count:
                continue
            total = part[i, owner]
            if s > 0:
                hop(i, slot + s - 1, device).wait_recv()
                total = total + sr[i, slot + s - 1].astype(F32)
            ss[i, slot + s] = total.astype(BF16)
            hop(i, slot + s, device).start()

    def deliver(i):
        j = (core * half + i) % CHUNKS
        place = pl.ds(pl.multiple_of(xl * wide + j * chunk, LANES), chunk)
        return remote(fo.at[i], out.at[:, place], o_send.at[i], o_recv.at[i], across)

    def delivered(i):
        j = (core * half + i) % CHUNKS
        place = pl.ds(pl.multiple_of((1 - xl) * wide + j * chunk, LANES), chunk)
        return remote(fo.at[i], out.at[:, place], o_send.at[i], o_recv.at[i], across)

    def finish(i, up, low):
        j = (core * half + i) % CHUNKS
        total = part[i, y]
        for slot, count, device in ((0, up, ahead), (up, low, behind)):
            if count:
                hop(i, slot + count - 1, device).wait_recv()
                total = total + sr[i, slot + count - 1].astype(F32)
        mine = jnp.where(xl == 0, total[: rows // 2], total[rows // 2 :])
        other = jnp.where(xl == 0, total[rows // 2 :], total[: rows // 2])
        fo[i] = other.astype(BF16)
        deliver(i).start()
        out[:, pl.ds(pl.multiple_of(xl * wide + j * chunk, LANES), chunk)] = mine.astype(BF16)

    def first(i, up, low):
        project(i, up, low)

    def second(i, up, low):
        forwarded(i - half).wait_recv()
        project(i, up, low)

    for i in range(half):
        first(i, *steps[i % 2])
    for i in range(half, CHUNKS):
        second(i, *steps[i % 2])
    for s in range(1, Y // 2):
        pairs(functools.partial(advance, s))
    pairs(finish)

    def drain(i, up, low):
        delivered(i).wait_recv()
        deliver(i).wait_send()
        for slot in range(Y - 1):
            hop(i, slot, ahead).wait_send()

    pairs(drain)
    exchange.wait_send()
    for i in range(half):
        direct(i).wait_send()
        forward(i).wait_send()
    each(lambda d: taps_copy(d).wait_send())
    each(lambda d: signal_copy(d).wait_send())
    each(lambda d: response_copy(d).wait_send())


def body(query, key_branch, value, filters, skip, weight):
    S = lax.axis_size("seq")
    T = lax.axis_size("tensor")
    Y = T // 2
    width = query.shape[1]
    columns = weight.shape[1]
    chunk = columns // 2 // CHUNKS
    rows = BLOCK // Y
    vmem = pl.BlockSpec(memory_space=pltpu.VMEM)
    dma = pltpu.SemaphoreType.DMA
    slabs = pltpu.VMEM((S, 2 * SLAB, LANES), BF16)
    return pl.pallas_call(
        functools.partial(kernel, S, Y),
        out_shape=jax.ShapeDtypeStruct((BLOCK // T, columns), BF16),
        in_specs=[vmem] * 5 + [pl.BlockSpec(memory_space=pl.ANY)],
        out_specs=vmem,
        scratch_shapes=[
            slabs, slabs,
            pltpu.VMEM((filters.shape[0], 2, LANES), F32), pltpu.VMEM((S, 2, LANES), F32),
            pltpu.VMEM((S + 1, 2, LANES, BLOCK), BF16),
            pltpu.VMEM((S * SLAB, UNROLL * BLOCK), BF16),
            pltpu.VMEM((S * SLAB, BLOCK), F32),
            slabs, slabs,
            pltpu.VMEM((BLOCK, width), BF16), pltpu.VMEM((BLOCK, width), BF16),
            pltpu.VMEM((2, CHUNKS, width, chunk), BF16),
            pltpu.VMEM((CHUNKS, Y, rows, chunk), F32),
            pltpu.VMEM((CHUNKS, Y - 1, rows, chunk), BF16),
            pltpu.VMEM((CHUNKS, Y - 1, rows, chunk), BF16),
            pltpu.VMEM((CHUNKS, rows // 2, chunk), BF16),
            dma((S,)), dma((S,)), dma((S,)), dma((S,)), dma((S,)), dma((S,)),
            dma((CHUNKS,)),
            dma((CHUNKS // 2,)), dma((CHUNKS // 2,)), dma((CHUNKS // 2,)), dma((CHUNKS // 2,)),
            dma((2,)),
            dma((CHUNKS, Y - 1)), dma((CHUNKS, Y - 1)),
            dma((CHUNKS,)), dma((CHUNKS,)),
        ],
        compiler_params=pltpu.CompilerParams(
            collective_id=0, has_side_effects=True, vmem_limit_bytes=48 * 2**20
        ),
        name="hyena",
    )(query, key_branch, value, filters, skip.reshape(1, width), weight)


def solution(mesh):
    return jax.shard_map(
        body,
        mesh=mesh,
        in_specs=(
            P("seq", "tensor"),
            P("seq", "tensor"),
            P("seq", "tensor"),
            P("tensor", "seq"),
            P("tensor"),
            P("tensor", None),
        ),
        out_specs=P(("seq", "tensor"), None),
        check_vma=False,
    )
```

```python
import functools

import jax
import jax.numpy as jnp
from jax import lax
from jax.experimental import pallas as pl
from jax.experimental.pallas import tpu as pltpu
from jax.sharding import PartitionSpec as P

F32 = jnp.float32
BF16 = jnp.bfloat16
LANES = 128
SLAB = 8
BLOCK = 2 * LANES
UNROLL = 4
CHUNKS = 8


def remote(src, dst, send, recv, device):
    return pltpu.make_async_remote_copy(
        src_ref=src,
        dst_ref=dst,
        send_sem=send,
        recv_sem=recv,
        device_id=device,
        device_id_type=pl.DeviceIdType.MESH,
    )


def kernel(
    S, Y,
    query_in, key_in, value_in, filters_in, skip_in, weight, out,
    query, key, value, filters, skip, i_sem,
    sx, rx, sq, rq, sf, rf, toeplitz, lhs, acc, sg, rg, gated, wv, part, ss, sr, fo,
    x_send, x_recv, q_send, q_recv, f_send, f_recv, g_send, g_recv,
    w_local, wd_send, wd_recv, wf_send, wf_recv, r_send, r_recv, o_send, o_recv,
):
    seq = lax.axis_index("seq")
    ten = lax.axis_index("tensor")
    y = ten // 2
    xl = ten % 2
    core = seq % 2
    across = (seq, ten + 1 - 2 * xl)
    around = (seq + 2 - 4 * (seq // 2 % 2), ten + 1 - 2 * xl)
    beside = (seq + 1 - 2 * core, ten)
    ahead = (seq, (ten + 2) % (2 * Y))
    behind = (seq, (ten + 2 * Y - 2) % (2 * Y))
    width = query.shape[1]
    columns = weight.shape[1]
    wide = columns // 2
    chunk = wide // CHUNKS
    half = CHUNKS // 2
    rows = BLOCK // Y

    inputs = [
        pltpu.make_async_copy(source, target, i_sem.at[n])
        for n, (source, target) in enumerate(
            ((key_in, key), (value_in, value), (filters_in, filters), (query_in, query), (skip_in, skip))
        )
    ]
    for copy in inputs:
        copy.start()

    barrier = pltpu.get_barrier_semaphore()

    def greet(device):
        pl.semaphore_signal(barrier, inc=1, device_id=device, device_id_type=pl.DeviceIdType.MESH)

    for device in (across, around, ahead, behind):
        greet(device)

    def greet_seq(d, _):
        greet(((seq + d) % S, ten))
        return 0

    lax.fori_loop(1, S, greet_seq, 0)

    def own_weight(j):
        return pltpu.make_async_copy(
            weight.at[:, pl.ds(pl.multiple_of(xl * wide + j * chunk, LANES), chunk)], wv.at[0, j], w_local.at[j]
        )

    for j in range(CHUNKS):
        own_weight(j).start()

    for copy in inputs:
        copy.wait()

    def slabs(array):
        turned = array.T
        return jnp.concatenate(
            [turned[:, :LANES].reshape(S, SLAB, LANES), turned[:, LANES:].reshape(S, SLAB, LANES)], axis=1
        ).astype(BF16)

    sx[...] = slabs(key[...].astype(F32) * value[...].astype(F32))
    for g in range(filters.shape[0]):
        for h in range(2):
            sf[g, h : h + 1, :] = filters[g : g + 1, h * LANES : (h + 1) * LANES]
    rx[pl.ds(seq, 1)] = sx[pl.ds(seq, 1)]
    rf[pl.ds(seq, 1)] = sf[pl.ds(seq // 2, 1)]

    pl.semaphore_wait(barrier, S + 3)

    def taps_copy(d):
        p = (seq + d) % S
        return remote(sf.at[p // 2], rf.at[seq], f_send.at[d], f_recv.at[d], (p, ten))

    def taps_wait(d):
        s = (seq + S - d) % S
        remote(sf.at[0], rf.at[s], f_send.at[d], f_recv.at[d], (s, ten)).wait_recv()

    def signal_copy(d):
        p = (seq + d) % S
        return remote(sx.at[p], rx.at[seq], x_send.at[d], x_recv.at[d], (p, ten))

    def signal_wait(d):
        s = (seq + S - d) % S
        remote(sx.at[s], rx.at[s], x_send.at[d], x_recv.at[d], (s, ten)).wait_recv()

    def query_copy(d):
        p = (seq + d) % S
        return remote(sq.at[p], rq.at[seq], q_send.at[d], q_recv.at[d], (p, ten))

    def query_wait(d):
        s = (seq + S - d) % S
        remote(sq.at[s], rq.at[s], q_send.at[d], q_recv.at[d], (s, ten)).wait_recv()

    def gated_copy(d, side):
        p = (seq + d) % S
        device = (p, ten) if side == 0 else (p, ten + 1 - 2 * xl)
        return remote(sg.at[p], rg.at[side, seq], g_send.at[side, d], g_recv.at[side, d], device)

    def gated_wait(d, side):
        s = (seq + S - d) % S
        device = (s, ten) if side == 0 else (s, ten + 1 - 2 * xl)
        remote(sg.at[s], rg.at[side, s], g_send.at[side, d], g_recv.at[side, d], device).wait_recv()

    def each(function):
        def step(d, _):
            function(d)
            return 0

        lax.fori_loop(1, S, step, 0)

    each(lambda d: taps_copy(d).start())
    each(lambda d: signal_copy(d).start())
    sq[...] = slabs(query[...].astype(F32))
    rq[pl.ds(seq, 1)] = sq[pl.ds(seq, 1)]
    each(lambda d: query_copy(d).start())

    def direct(i):
        j = core * half + i
        return remote(
            weight.at[:, pl.ds(pl.multiple_of((1 - xl) * wide + j * chunk, LANES), chunk)],
            wv.at[1, j], wd_send.at[i], wd_recv.at[i], across if i % 2 == 0 else around,
        )

    def forward(i):
        j = core * half + i
        return remote(wv.at[1, j], wv.at[1, j], wf_send.at[i], wf_recv.at[i], beside)

    def forwarded(i):
        j = (1 - core) * half + i
        return remote(wv.at[1, j], wv.at[1, j], wf_send.at[i], wf_recv.at[i], beside)

    for i in range(half):
        direct(i).start()

    each(taps_wait)
    toeplitz[0, 1, :, 0:LANES] = jnp.zeros((LANES, LANES), BF16)
    lane = lax.broadcasted_iota(jnp.int32, (LANES, LANES), 1)
    down = lax.broadcasted_iota(jnp.int32, (LANES, LANES), 0)
    mask = lane >= down

    def build(a, before):
        for h in range(2):
            row = jnp.broadcast_to(rf[a, h : h + 1, :], (LANES, LANES))
            rolled = pltpu.roll(row, 0, 1, stride=1, stride_axis=0)
            block = jnp.where(mask, rolled, before).astype(BF16)
            before = rolled
            if h == 0:
                toeplitz[a, 0, :, 0:LANES] = block
                toeplitz[a, 1, :, LANES:BLOCK] = block
            else:
                toeplitz[a, 0, :, LANES:BLOCK] = block
                toeplitz[a + 1, 1, :, 0:LANES] = block
        return before

    lax.fori_loop(0, S, build, jnp.zeros((LANES, LANES), F32), unroll=4)

    each(signal_wait)
    signal = rx[...].astype(F32)
    for h in range(2):
        piece = signal[:, h * SLAB : (h + 1) * SLAB, :].reshape(S * SLAB, LANES)
        for r in range(UNROLL):
            shifted = piece
            if r > 0:
                shifted = jnp.concatenate([jnp.zeros((r * SLAB, LANES), F32), piece[: (S - r) * SLAB]], axis=0)
            lhs[:, r * BLOCK + h * LANES : r * BLOCK + (h + 1) * LANES] = shifted.astype(BF16)
    for step in range(S // UNROLL):
        top = step * UNROLL * SLAB
        taps = toeplitz[step * UNROLL : (step + 1) * UNROLL].reshape(UNROLL * BLOCK, BLOCK)
        product = jnp.dot(lhs[: S * SLAB - top, :], taps, preferred_element_type=F32)
        if step == 0:
            acc[...] = product
        else:
            acc[top:, :] += product
    each(query_wait)
    spot = lax.broadcasted_iota(jnp.int32, (SLAB, width), 1) - SLAB * seq
    picked = spot == lax.broadcasted_iota(jnp.int32, (SLAB, width), 0)
    direct_term = jnp.sum(jnp.where(picked, skip[...], 0.0), axis=1, keepdims=True)
    pieces = []
    for h in range(2):
        span = slice(h * SLAB, (h + 1) * SLAB)
        response = acc[:, h * LANES : (h + 1) * LANES].reshape(S, SLAB, LANES)
        term = response + direct_term[None] * rx[...].astype(F32)[:, span]
        pieces.append(rq[...].astype(F32)[:, span] * term)
    sg[...] = jnp.concatenate(pieces, axis=1).astype(BF16)

    def send_gated(d):
        gated_copy(d, 0).start()
        gated_copy(d, 1).start()

    each(send_gated)
    gated_copy(0, 1).start()
    rg[0, pl.ds(seq, 1)] = sg[pl.ds(seq, 1)]

    for i in range(half // 2):
        direct(i).wait_recv()
        forward(i).start()
    for j in range(CHUNKS):
        own_weight(j).wait()

    def wait_gated(d):
        gated_wait(d, 0)
        gated_wait(d, 1)

    each(wait_gated)
    gated_wait(0, 1)
    for side in range(2):
        for h in range(2):
            piece = rg[side].astype(F32)[:, h * SLAB : (h + 1) * SLAB].reshape(width, LANES)
            gated[side, h * LANES : (h + 1) * LANES, :] = piece.T.astype(BF16)
    for i in range(half // 2, half):
        direct(i).wait_recv()
        forward(i).start()

    steps = [((Y - 1) // 2, Y // 2), (Y // 2, (Y - 1) // 2)]

    def hop(i, slot, device):
        return remote(ss.at[i, slot], sr.at[i, slot], r_send.at[i, slot], r_recv.at[i, slot], device)

    def chunk_of(i, parity):
        return (core + parity) % 2 * half + i // 2

    def pairs(function):
        def step(pair, _):
            for parity in range(2):
                function(2 * pair + parity, parity)
            return 0

        lax.fori_loop(0, half, step, 0)

    def project(i, parity):
        j = chunk_of(i, parity)
        term = jnp.dot(gated[0], wv[0, j], preferred_element_type=F32)
        term = term + jnp.dot(gated[1], wv[1, j], preferred_element_type=F32)
        part[i] = term.reshape(Y, rows, chunk)
        advance(0, i, parity)

    def advance(s, i, parity):
        up, low = steps[parity]
        for slot, count, device, owner in (
            (0, up, ahead, (y + up - s) % Y),
            (up, low, behind, (y + Y - low + s) % Y),
        ):
            if s >= count:
                continue
            total = part[i, owner]
            if s > 0:
                hop(i, slot + s - 1, device).wait_recv()
                total = total + sr[i, slot + s - 1].astype(F32)
            ss[i, slot + s] = total.astype(BF16)
            hop(i, slot + s, device).start()

    def deliver(i, parity):
        j = chunk_of(i, parity)
        place = pl.ds(pl.multiple_of(xl * wide + j * chunk, LANES), chunk)
        return remote(fo.at[i], out.at[:, place], o_send.at[i], o_recv.at[i], across)

    def delivered(i, parity):
        j = chunk_of(i, parity)
        place = pl.ds(pl.multiple_of((1 - xl) * wide + j * chunk, LANES), chunk)
        return remote(fo.at[i], out.at[:, place], o_send.at[i], o_recv.at[i], across)

    def finish(i, parity):
        up, low = steps[parity]
        j = chunk_of(i, parity)
        total = part[i, y]
        for slot, count, device in ((0, up, ahead), (up, low, behind)):
            if count:
                hop(i, slot + count - 1, device).wait_recv()
                total = total + sr[i, slot + count - 1].astype(F32)
        mine = jnp.where(xl == 0, total[: rows // 2], total[rows // 2 :])
        other = jnp.where(xl == 0, total[rows // 2 :], total[: rows // 2])
        fo[i] = other.astype(BF16)
        deliver(i, parity).start()
        out[:, pl.ds(pl.multiple_of(xl * wide + j * chunk, LANES), chunk)] = mine.astype(BF16)

    for i in range(CHUNKS):
        if i % 2 == 1:
            forwarded(i // 2).wait_recv()
        project(i, i % 2)
    each(lambda d: taps_copy(d).wait_send())
    each(lambda d: signal_copy(d).wait_send())
    each(lambda d: query_copy(d).wait_send())
    for s in range(1, Y // 2):
        pairs(functools.partial(advance, s))
        if s == 1:
            each(lambda d: gated_copy(d, 0).wait_send())
            each(lambda d: gated_copy(d, 1).wait_send())
            gated_copy(0, 1).wait_send()
    pairs(finish)

    def drain(i, parity):
        delivered(i, parity).wait_recv()
        deliver(i, parity).wait_send()
        for slot in range(Y - 1):
            hop(i, slot, ahead).wait_send()

    pairs(drain)
    for i in range(half):
        direct(i).wait_send()
        forward(i).wait_send()


def body(query, key_branch, value, filters, skip, weight):
    S = lax.axis_size("seq")
    T = lax.axis_size("tensor")
    Y = T // 2
    width = query.shape[1]
    columns = weight.shape[1]
    chunk = columns // 2 // CHUNKS
    rows = BLOCK // Y
    vmem = pl.BlockSpec(memory_space=pltpu.VMEM)
    dma = pltpu.SemaphoreType.DMA
    slab = pltpu.VMEM((S, 2 * SLAB, LANES), BF16)
    return pl.pallas_call(
        functools.partial(kernel, S, Y),
        out_shape=jax.ShapeDtypeStruct((BLOCK // T, columns), BF16),
        in_specs=[pl.BlockSpec(memory_space=pltpu.HBM)] * 6,
        out_specs=vmem,
        scratch_shapes=[
            pltpu.VMEM(query.shape, BF16), pltpu.VMEM(query.shape, BF16), pltpu.VMEM(query.shape, BF16),
            pltpu.VMEM(filters.shape, F32), pltpu.VMEM((1, width), F32), dma((5,)),
            slab, slab, slab, slab,
            pltpu.VMEM((filters.shape[0], 2, LANES), F32), pltpu.VMEM((S, 2, LANES), F32),
            pltpu.VMEM((S + 1, 2, LANES, BLOCK), BF16),
            pltpu.VMEM((S * SLAB, UNROLL * BLOCK), BF16),
            pltpu.VMEM((S * SLAB, BLOCK), F32),
            slab, pltpu.VMEM((2, S, 2 * SLAB, LANES), BF16),
            pltpu.VMEM((2, BLOCK, width), BF16),
            pltpu.VMEM((2, CHUNKS, width, chunk), BF16),
            pltpu.VMEM((CHUNKS, Y, rows, chunk), F32),
            pltpu.VMEM((CHUNKS, Y - 1, rows, chunk), BF16),
            pltpu.VMEM((CHUNKS, Y - 1, rows, chunk), BF16),
            pltpu.VMEM((CHUNKS, rows // 2, chunk), BF16),
            dma((S,)), dma((S,)), dma((S,)), dma((S,)), dma((S,)), dma((S,)), dma((2, S)), dma((2, S)),
            dma((CHUNKS,)),
            dma((CHUNKS // 2,)), dma((CHUNKS // 2,)), dma((CHUNKS // 2,)), dma((CHUNKS // 2,)),
            dma((CHUNKS, Y - 1)), dma((CHUNKS, Y - 1)),
            dma((CHUNKS,)), dma((CHUNKS,)),
        ],
        compiler_params=pltpu.CompilerParams(
            collective_id=0, has_side_effects=True, vmem_limit_bytes=60 * 2**20
        ),
        name="hyena",
    )(query, key_branch, value, filters, skip.reshape(1, width), weight)


def solution(mesh):
    return jax.shard_map(
        body,
        mesh=mesh,
        in_specs=(
            P("seq", "tensor"),
            P("seq", "tensor"),
            P("seq", "tensor"),
            P("tensor", "seq"),
            P("tensor"),
            P("tensor", None),
        ),
        out_specs=P(("seq", "tensor"), None),
        check_vma=False,
    )
```

```python
import functools

import jax
import jax.numpy as jnp
from jax import lax
from jax.experimental import pallas as pl
from jax.experimental.pallas import tpu as pltpu
from jax.sharding import PartitionSpec as P

F32 = jnp.float32
BF16 = jnp.bfloat16
LANES = 128
GROUPS_OF_SLABS = 4
SLAB = 8
BLOCK = 2 * LANES
UNROLL = 4
CHUNKS = 8


def remote(src, dst, send, recv, device):
    return pltpu.make_async_remote_copy(
        src_ref=src,
        dst_ref=dst,
        send_sem=send,
        recv_sem=recv,
        device_id=device,
        device_id_type=pl.DeviceIdType.MESH,
    )


def kernel(
    S, Y,
    query_in, key_in, value_in, filters_in, skip_in, weight, out,
    factors, filters, skip, i_sem,
    sx, rx, sq, sf, rf, toeplitz, lhs, acc, sg, rg, gk, gx, gs, gated, wv, part, ss, sr, fo,
    x_send, x_recv, f_send, f_recv, g_send, g_recv, e_send, e_recv,
    w_local, wd_send, wd_recv, wf_send, wf_recv, r_send, r_recv, o_send, o_recv,
):
    seq = lax.axis_index("seq")
    ten = lax.axis_index("tensor")
    y = ten // 2
    xl = ten % 2
    core = seq % 2
    across = (seq, ten + 1 - 2 * xl)
    around = (seq + 2 - 4 * (seq // 2 % 2), ten + 1 - 2 * xl)
    beside = (seq + 1 - 2 * core, ten)
    ahead = (seq, (ten + 2) % (2 * Y))
    behind = (seq, (ten + 2 * Y - 2) % (2 * Y))
    width = factors.shape[2]
    columns = weight.shape[1]
    wide = columns // 2
    chunk = wide // CHUNKS
    half = CHUNKS // 2
    rows = BLOCK // Y
    group = S // GROUPS_OF_SLABS

    inputs = [
        pltpu.make_async_copy(key_in, factors.at[0], i_sem.at[0]),
        pltpu.make_async_copy(value_in, factors.at[1], i_sem.at[0]),
        pltpu.make_async_copy(query_in, factors.at[2], i_sem.at[0]),
        pltpu.make_async_copy(filters_in, filters, i_sem.at[1]),
        pltpu.make_async_copy(skip_in, skip, i_sem.at[2]),
    ]
    for copy in inputs:
        copy.start()

    barrier = pltpu.get_barrier_semaphore()

    def greet(device):
        pl.semaphore_signal(barrier, inc=1, device_id=device, device_id_type=pl.DeviceIdType.MESH)

    for device in (across, around, ahead, behind):
        greet(device)

    def greet_seq(d, _):
        greet(((seq + d) % S, ten))
        return 0

    lax.fori_loop(1, S, greet_seq, 0)

    def own_weight(j):
        return pltpu.make_async_copy(
            weight.at[:, pl.ds(pl.multiple_of(xl * wide + j * chunk, LANES), chunk)], wv.at[0, j], w_local.at[0]
        )

    for j in range(CHUNKS):
        own_weight(j).start()

    pltpu.make_async_copy(factors, factors, i_sem.at[0]).wait()
    inputs[3].wait()
    inputs[4].wait()

    def slabs(array):
        turned = array.T
        return jnp.concatenate(
            [turned[:, :LANES].reshape(S, SLAB, LANES), turned[:, LANES:].reshape(S, SLAB, LANES)], axis=1
        ).astype(BF16)

    sx[...] = slabs(factors[0].astype(F32) * factors[1].astype(F32))
    for g in range(filters.shape[0]):
        for h in range(2):
            sf[g, h : h + 1, :] = filters[g : g + 1, h * LANES : (h + 1) * LANES]
    rx[pl.ds(seq, 1)] = sx[pl.ds(seq, 1)]
    rf[pl.ds(seq, 1)] = sf[pl.ds(seq // 2, 1)]

    pl.semaphore_wait(barrier, S + 3)

    def taps_copy(k):
        p = (seq + S - k) % S
        return remote(sf.at[p // 2], rf.at[seq], f_send.at[0], f_recv.at[0], (p, ten))

    def signal_copy(k):
        p = (seq + S - k) % S
        return remote(sx.at[p], rx.at[seq], x_send.at[0], x_recv.at[0], (p, ten))

    def response_copy(k):
        p = (seq + S - k) % S
        return remote(sg.at[p], rg.at[k], g_send.at[0], g_recv.at[k // group], (p, ten))

    def relay(n):
        span = pl.ds(n * group, group)
        return remote(gk.at[span], gx.at[span], e_send.at[0], e_recv.at[n], across)

    order = [GROUPS_OF_SLABS // 2, GROUPS_OF_SLABS // 2 - 1] + list(range(GROUPS_OF_SLABS // 2 + 1, GROUPS_OF_SLABS)) + [0]

    def each_of(n, function):
        def step(k, _):
            function(k)
            return 0

        lax.fori_loop(max(n * group, 1), (n + 1) * group, step, 0)

    def each(function):
        for n in order:
            each_of(n, function)

    each(lambda k: taps_copy(k).start())
    each(lambda k: signal_copy(k).start())
    sq[...] = slabs(factors[2].astype(F32))

    def direct(i):
        j = core * half + i
        return remote(
            weight.at[:, pl.ds(pl.multiple_of((1 - xl) * wide + j * chunk, LANES), chunk)],
            wv.at[1, j], wd_send.at[0], wd_recv.at[i], across if i % 2 == 0 else around,
        )

    def forward(i):
        j = core * half + i
        return remote(wv.at[1, j], wv.at[1, j], wf_send.at[0], wf_recv.at[i], beside)

    def forwarded(i):
        j = (1 - core) * half + i
        return remote(wv.at[1, j], wv.at[1, j], wf_send.at[0], wf_recv.at[i], beside)

    for i in range(half):
        direct(i).start()

    everyone = pl.ds(0, S - 1)
    all_taps = remote(rf.at[everyone], rf.at[everyone], f_send.at[0], f_recv.at[0], across)
    all_signals = remote(rx.at[everyone], rx.at[everyone], x_send.at[0], x_recv.at[0], across)
    all_responses = remote(sg.at[everyone], rg.at[everyone], g_send.at[0], g_recv.at[0], across)
    all_relays = remote(gk, gx, e_send.at[0], e_recv.at[0], across)

    def some_responses(n):
        span = pl.ds(0, group if n > 0 else group - 1)
        return remote(sg.at[span], rg.at[span], g_send.at[0], g_recv.at[n], across)

    all_taps.wait_recv()
    toeplitz[0, 1, :, 0:LANES] = jnp.zeros((LANES, LANES), BF16)
    lane = lax.broadcasted_iota(jnp.int32, (LANES, LANES), 1)
    down = lax.broadcasted_iota(jnp.int32, (LANES, LANES), 0)
    mask = lane >= down

    def build(a, before):
        for h in range(2):
            row = jnp.broadcast_to(rf[a, h : h + 1, :], (LANES, LANES))
            rolled = pltpu.roll(row, 0, 1, stride=1, stride_axis=0)
            block = jnp.where(mask, rolled, before).astype(BF16)
            before = rolled
            if h == 0:
                toeplitz[a, 0, :, 0:LANES] = block
                toeplitz[a, 1, :, LANES:BLOCK] = block
            else:
                toeplitz[a, 0, :, LANES:BLOCK] = block
                toeplitz[a + 1, 1, :, 0:LANES] = block
        return before

    lax.fori_loop(0, S, build, jnp.zeros((LANES, LANES), F32), unroll=4)

    all_signals.wait_recv()
    signal = rx[...].astype(F32)
    for h in range(2):
        piece = signal[:, h * SLAB : (h + 1) * SLAB, :].reshape(S * SLAB, LANES)
        for r in range(UNROLL):
            shifted = piece
            if r > 0:
                shifted = jnp.concatenate([jnp.zeros((r * SLAB, LANES), F32), piece[: (S - r) * SLAB]], axis=0)
            lhs[:, r * BLOCK + h * LANES : r * BLOCK + (h + 1) * LANES] = shifted.astype(BF16)
    for step in range(S // UNROLL):
        top = step * UNROLL * SLAB
        taps = toeplitz[step * UNROLL : (step + 1) * UNROLL].reshape(UNROLL * BLOCK, BLOCK)
        product = jnp.dot(lhs[: S * SLAB - top, :], taps, preferred_element_type=F32)
        if step == 0:
            acc[...] = product
        else:
            acc[top:, :] += product
    spot = lax.broadcasted_iota(jnp.int32, (SLAB, width), 1) - SLAB * seq
    picked = spot == lax.broadcasted_iota(jnp.int32, (SLAB, width), 0)
    scale = jnp.sum(jnp.where(picked, skip[...], 0.0), axis=1, keepdims=True)
    pieces = []
    for h in range(2):
        response = acc[:, h * LANES : (h + 1) * LANES].reshape(S, SLAB, LANES)
        pieces.append(response + scale[None] * rx[...].astype(F32)[:, h * SLAB : (h + 1) * SLAB])
    sg[...] = jnp.concatenate(pieces, axis=1).astype(BF16)
    each(lambda k: response_copy(k).start())
    rg[pl.ds(0, 1)] = sg[pl.ds(seq, 1)]

    for i in range(half // 2):
        direct(i).wait_recv()
        forward(i).start()
    pltpu.make_async_copy(wv.at[0], wv.at[0], w_local.at[0]).wait()

    def turn(side):
        for h in range(2):
            piece = gs[...].astype(F32)[:, h * SLAB : (h + 1) * SLAB].reshape(width, LANES)
            gated[side, h * LANES : (h + 1) * LANES, :] = piece.T.astype(BF16)

    for n in order:
        some_responses(n).wait_recv()
        for k in range(n * group, (n + 1) * group):
            s = (seq + k) % S
            slab = (sq[s].astype(F32) * rg[k].astype(F32)).astype(BF16)
            gk[k] = slab
            gs[s] = slab
        relay(n).start()
    turn(0)

    def chunk_of(i, parity):
        return (core + parity) % 2 * half + i // 2

    for i in range(CHUNKS):
        term = jnp.dot(gated[0], wv[0, chunk_of(i, i % 2)], preferred_element_type=F32)
        part[i] = term.reshape(Y, rows, chunk)
    for n in order:
        relay(n).wait_recv()
    for k in range(S):
        gs[(seq + k) % S] = gx[k]
    turn(1)

    steps = [((Y - 1) // 2, Y // 2), (Y // 2, (Y - 1) // 2)]

    def hop(i, slot, device):
        return remote(ss.at[i, slot], sr.at[i, slot], r_send.at[0], r_recv.at[i, slot], device)

    def pairs(batch, function):
        def step(pair, _):
            for parity in range(2):
                function(2 * pair + parity, parity)
            return 0

        lax.fori_loop(batch * half // 2, (batch + 1) * half // 2, step, 0)

    def project(i, parity):
        j = chunk_of(i, parity)
        term = jnp.dot(gated[1], wv[1, j], preferred_element_type=F32)
        part[i] += term.reshape(Y, rows, chunk)
        advance(0, i, parity)

    def advance(s, i, parity):
        up, low = steps[parity]
        for slot, count, device, owner in (
            (0, up, ahead, (y + up - s) % Y),
            (up, low, behind, (y + Y - low + s) % Y),
        ):
            if s >= count:
                continue
            total = part[i, owner]
            if s > 0:
                hop(i, slot + s - 1, device).wait_recv()
                total = total + sr[i, slot + s - 1].astype(F32)
            ss[i, slot + s] = total.astype(BF16)
            hop(i, slot + s, device).start()

    def deliver(i, parity):
        j = chunk_of(i, parity)
        place = pl.ds(pl.multiple_of(xl * wide + j * chunk, LANES), chunk)
        return remote(fo.at[i], out.at[:, place], o_send.at[0], o_recv.at[0], across)

    def finish(i, parity):
        up, low = steps[parity]
        j = chunk_of(i, parity)
        total = part[i, y]
        for slot, count, device in ((0, up, ahead), (up, low, behind)):
            if count:
                hop(i, slot + count - 1, device).wait_recv()
                total = total + sr[i, slot + count - 1].astype(F32)
        mine = jnp.where(xl == 0, total[: rows // 2], total[rows // 2 :])
        other = jnp.where(xl == 0, total[rows // 2 :], total[: rows // 2])
        fo[i] = other.astype(BF16)
        deliver(i, parity).start()
        out[:, pl.ds(pl.multiple_of(xl * wide + j * chunk, LANES), chunk)] = mine.astype(BF16)

    for i in range(half):
        if i % 2 == 1:
            forwarded(i // 2).wait_recv()
        project(i, i % 2)
    all_taps.wait_send()
    all_signals.wait_send()
    all_responses.wait_send()
    all_relays.wait_send()
    for n in range(half // 2, half):
        direct(n).wait_recv()
        forward(n).start()
    pairs(0, functools.partial(advance, 1))
    for i in range(half, CHUNKS):
        if i % 2 == 1:
            forwarded(i // 2).wait_recv()
        project(i, i % 2)
    for s in range(2, Y // 2):
        pairs(0, functools.partial(advance, s))
        pairs(1, functools.partial(advance, s - 1))
    pairs(0, finish)
    if Y // 2 > 1:
        pairs(1, functools.partial(advance, Y // 2 - 1))
    pairs(1, finish)

    remote(wv.at[0, pl.ds(0, half)], wv.at[0, pl.ds(0, half)], wd_send.at[0], wd_recv.at[0], across).wait_send()
    remote(wv.at[1, pl.ds(0, half)], wv.at[1, pl.ds(0, half)], wf_send.at[0], wf_recv.at[0], beside).wait_send()
    remote(ss, sr, r_send.at[0], r_recv.at[0, 0], ahead).wait_send()
    other = out.at[:, pl.ds(pl.multiple_of((1 - xl) * wide, LANES), wide)]
    delivered = remote(other, other, o_send.at[0], o_recv.at[0], across)
    delivered.wait_send()
    delivered.wait_recv()


def body(query, key_branch, value, filters, skip, weight):
    S = lax.axis_size("seq")
    T = lax.axis_size("tensor")
    Y = T // 2
    width = query.shape[1]
    columns = weight.shape[1]
    chunk = columns // 2 // CHUNKS
    rows = BLOCK // Y
    vmem = pl.BlockSpec(memory_space=pltpu.VMEM)
    dma = pltpu.SemaphoreType.DMA
    slab = pltpu.VMEM((S, 2 * SLAB, LANES), BF16)
    return pl.pallas_call(
        functools.partial(kernel, S, Y),
        out_shape=jax.ShapeDtypeStruct((BLOCK // T, columns), BF16),
        in_specs=[pl.BlockSpec(memory_space=pltpu.HBM)] * 6,
        out_specs=vmem,
        scratch_shapes=[
            pltpu.VMEM((3, *query.shape), BF16), pltpu.VMEM(filters.shape, F32), pltpu.VMEM((1, width), F32), dma((3,)),
            slab, slab, slab,
            pltpu.VMEM((filters.shape[0], 2, LANES), F32), pltpu.VMEM((S, 2, LANES), F32),
            pltpu.VMEM((S + 1, 2, LANES, BLOCK), BF16),
            pltpu.VMEM((S * SLAB, UNROLL * BLOCK), BF16),
            pltpu.VMEM((S * SLAB, BLOCK), F32),
            slab, slab, slab, slab, slab,
            pltpu.VMEM((2, BLOCK, width), BF16),
            pltpu.VMEM((2, CHUNKS, width, chunk), BF16),
            pltpu.VMEM((CHUNKS, Y, rows, chunk), F32),
            pltpu.VMEM((CHUNKS, Y - 1, rows, chunk), BF16),
            pltpu.VMEM((CHUNKS, Y - 1, rows, chunk), BF16),
            pltpu.VMEM((CHUNKS, rows // 2, chunk), BF16),
            dma((1,)), dma((1,)), dma((1,)), dma((1,)), dma((1,)), dma((GROUPS_OF_SLABS,)),
            dma((1,)), dma((GROUPS_OF_SLABS,)),
            dma((1,)),
            dma((1,)), dma((CHUNKS // 2,)), dma((1,)), dma((CHUNKS // 2,)),
            dma((1,)), dma((CHUNKS, Y - 1)),
            dma((1,)), dma((1,)),
        ],
        compiler_params=pltpu.CompilerParams(
            collective_id=0, has_side_effects=True, vmem_limit_bytes=60 * 2**20
        ),
        name="hyena",
    )(query, key_branch, value, filters, skip.reshape(1, width), weight)


def solution(mesh):
    return jax.shard_map(
        body,
        mesh=mesh,
        in_specs=(
            P("seq", "tensor"),
            P("seq", "tensor"),
            P("seq", "tensor"),
            P("tensor", "seq"),
            P("tensor"),
            P("tensor", None),
        ),
        out_specs=P(("seq", "tensor"), None),
        check_vma=False,
    )
```

```python
import functools

import jax
import jax.numpy as jnp
from jax import lax
from jax.experimental import pallas as pl
from jax.experimental.pallas import tpu as pltpu
from jax.sharding import PartitionSpec as P

F32 = jnp.float32
BF16 = jnp.bfloat16
LANES = 128
GROUPS_OF_SLABS = 4
SLAB = 8
BLOCK = 2 * LANES
UNROLL = 4
CHUNKS = 8


def remote(src, dst, send, recv, device):
    return pltpu.make_async_remote_copy(
        src_ref=src,
        dst_ref=dst,
        send_sem=send,
        recv_sem=recv,
        device_id=device,
        device_id_type=pl.DeviceIdType.MESH,
    )


def kernel(
    S, Y,
    query_in, key_in, value_in, filters_in, skip_in, weight, out,
    factors, filters, skip, i_sem,
    sx, rx, sq, sf, rf, toeplitz, lhs, acc, sg, rg, gk, gx, gs, qx, hx, gated, wv, part, ss, sr, lr, fo, fr, result,
    x_send, x_recv, f_send, f_recv, g_send, g_recv, e_send, e_recv, h_send, h_recv,
    w_local, wd_send, wd_recv, wf_send, wf_recv, r_send, r_recv, l_recv, p_sem, o_sem,
):
    seq = lax.axis_index("seq")
    ten = lax.axis_index("tensor")
    y = ten // 2
    xl = ten % 2
    core = seq % 2
    across = (seq, ten + 1 - 2 * xl)
    around = (seq + 2 - 4 * (seq // 2 % 2), ten + 1 - 2 * xl)
    beside = (seq + 1 - 2 * core, ten)
    ahead = (seq, (ten + 2) % (2 * Y))
    behind = (seq, (ten + 2 * Y - 2) % (2 * Y))
    neighbours = ((ahead, (seq, (ten + 3 - 2 * xl) % (2 * Y))), (behind, (seq, (ten + 2 * Y - 1 - 2 * xl) % (2 * Y))))
    width = factors.shape[2]
    columns = weight.shape[1]
    wide = columns // 2
    chunk = wide // CHUNKS
    half = CHUNKS // 2
    rows = BLOCK // Y
    group = S // GROUPS_OF_SLABS

    inputs = [
        pltpu.make_async_copy(key_in, factors.at[0], i_sem.at[0]),
        pltpu.make_async_copy(value_in, factors.at[1], i_sem.at[0]),
        pltpu.make_async_copy(query_in, factors.at[2], i_sem.at[0]),
        pltpu.make_async_copy(filters_in, filters, i_sem.at[1]),
        pltpu.make_async_copy(skip_in, skip, i_sem.at[2]),
    ]
    for copy in inputs:
        copy.start()

    barrier = pltpu.get_barrier_semaphore()

    def greet(device):
        pl.semaphore_signal(barrier, inc=1, device_id=device, device_id_type=pl.DeviceIdType.MESH)

    for device in (across, around, *neighbours[0], *neighbours[1]):
        greet(device)

    def greet_seq(d, _):
        greet(((seq + d) % S, ten))
        return 0

    lax.fori_loop(1, S, greet_seq, 0)
    for k in range(1, group):
        greet(((seq + k) % S, ten + 1 - 2 * xl))

    def own_weight(j):
        return pltpu.make_async_copy(
            weight.at[:, pl.ds(pl.multiple_of(xl * wide + j * chunk, LANES), chunk)], wv.at[0, j], w_local.at[0]
        )

    for j in range(CHUNKS):
        own_weight(j).start()

    pltpu.make_async_copy(factors, factors, i_sem.at[0]).wait()
    inputs[3].wait()
    inputs[4].wait()

    def slabs(array):
        turned = array.T
        return jnp.concatenate(
            [turned[:, :LANES].reshape(S, SLAB, LANES), turned[:, LANES:].reshape(S, SLAB, LANES)], axis=1
        ).astype(BF16)

    sx[...] = slabs(factors[0].astype(F32) * factors[1].astype(F32))
    for g in range(filters.shape[0]):
        for h in range(2):
            sf[g, h : h + 1, :] = filters[g : g + 1, h * LANES : (h + 1) * LANES]
    rx[pl.ds(seq, 1)] = sx[pl.ds(seq, 1)]
    rf[pl.ds(seq, 1)] = sf[pl.ds(seq // 2, 1)]

    pl.semaphore_wait(barrier, S + 4 + group)

    def taps_copy(k):
        p = (seq + S - k) % S
        return remote(sf.at[p // 2], rf.at[seq], f_send.at[0], f_recv.at[0], (p, ten))

    def signal_copy(k):
        p = (seq + S - k) % S
        return remote(sx.at[p], rx.at[seq], x_send.at[0], x_recv.at[0], (p, ten))

    def response_copy(k):
        p = (seq + S - k) % S
        return remote(sg.at[p], rg.at[k], g_send.at[0], g_recv.at[k // group], (p, ten))

    def twin_copy(k):
        p = (seq + S - k) % S
        return remote(sg.at[p], hx.at[k], h_send.at[0], h_recv.at[0], (p, ten + 1 - 2 * xl))

    def relay(n):
        span = pl.ds(n * group, group)
        return remote(gk.at[span], gx.at[span], e_send.at[0], e_recv.at[n], across)

    order = [GROUPS_OF_SLABS // 2, GROUPS_OF_SLABS // 2 - 1] + list(range(GROUPS_OF_SLABS // 2 + 1, GROUPS_OF_SLABS)) + [0]

    def each_of(n, function):
        def step(k, _):
            function(k)
            return 0

        lax.fori_loop(max(n * group, 1), (n + 1) * group, step, 0)

    def each(function):
        for n in order:
            each_of(n, function)

    each(lambda k: taps_copy(k).start())
    each(lambda k: signal_copy(k).start())
    sq[...] = slabs(factors[2].astype(F32))
    for k in range(group):
        remote(sq.at[(seq + k) % S], qx.at[k], h_send.at[1], h_recv.at[1], across).start()

    def direct(i):
        j = core * half + i
        return remote(
            weight.at[:, pl.ds(pl.multiple_of((1 - xl) * wide + j * chunk, LANES), chunk)],
            wv.at[1, j], wd_send.at[0], wd_recv.at[i], across if i % 2 == 0 else around,
        )

    def forward(i):
        j = core * half + i
        return remote(wv.at[1, j], wv.at[1, j], wf_send.at[0], wf_recv.at[i], beside)

    def forwarded(i):
        j = (1 - core) * half + i
        return remote(wv.at[1, j], wv.at[1, j], wf_send.at[0], wf_recv.at[i], beside)

    for i in range(half):
        direct(i).start()

    everyone = pl.ds(0, S - 1)
    all_taps = remote(rf.at[everyone], rf.at[everyone], f_send.at[0], f_recv.at[0], across)
    all_signals = remote(rx.at[everyone], rx.at[everyone], x_send.at[0], x_recv.at[0], across)
    all_responses = remote(sg.at[everyone], rg.at[everyone], g_send.at[0], g_recv.at[0], across)
    far = pl.ds(group, S - group)
    all_relays = remote(gk.at[far], gx.at[far], e_send.at[0], e_recv.at[0], across)
    all_twins = remote(hx, hx, h_send.at[0], h_recv.at[0], across)

    def some_responses(n):
        span = pl.ds(0, group if n > 0 else group - 1)
        return remote(sg.at[span], rg.at[span], g_send.at[0], g_recv.at[n], across)

    all_taps.wait_recv()
    toeplitz[0, 1, :, 0:LANES] = jnp.zeros((LANES, LANES), BF16)
    lane = lax.broadcasted_iota(jnp.int32, (LANES, LANES), 1)
    down = lax.broadcasted_iota(jnp.int32, (LANES, LANES), 0)
    mask = lane >= down

    def build(a, before):
        for h in range(2):
            row = jnp.broadcast_to(rf[a, h : h + 1, :], (LANES, LANES))
            rolled = pltpu.roll(row, 0, 1, stride=1, stride_axis=0)
            block = jnp.where(mask, rolled, before).astype(BF16)
            before = rolled
            if h == 0:
                toeplitz[a, 0, :, 0:LANES] = block
                toeplitz[a, 1, :, LANES:BLOCK] = block
            else:
                toeplitz[a, 0, :, LANES:BLOCK] = block
                toeplitz[a + 1, 1, :, 0:LANES] = block
        return before

    lax.fori_loop(0, S, build, jnp.zeros((LANES, LANES), F32), unroll=4)

    all_signals.wait_recv()
    signal = rx[...].astype(F32)
    for h in range(2):
        piece = signal[:, h * SLAB : (h + 1) * SLAB, :].reshape(S * SLAB, LANES)
        for r in range(UNROLL):
            shifted = piece
            if r > 0:
                shifted = jnp.concatenate([jnp.zeros((r * SLAB, LANES), F32), piece[: (S - r) * SLAB]], axis=0)
            lhs[:, r * BLOCK + h * LANES : r * BLOCK + (h + 1) * LANES] = shifted.astype(BF16)
    for step in range(S // UNROLL):
        top = step * UNROLL * SLAB
        taps = toeplitz[step * UNROLL : (step + 1) * UNROLL].reshape(UNROLL * BLOCK, BLOCK)
        product = jnp.dot(lhs[: S * SLAB - top, :], taps, preferred_element_type=F32)
        if step == 0:
            acc[...] = product
        else:
            acc[top:, :] += product
    spot = lax.broadcasted_iota(jnp.int32, (SLAB, width), 1) - SLAB * seq
    picked = spot == lax.broadcasted_iota(jnp.int32, (SLAB, width), 0)
    scale = jnp.sum(jnp.where(picked, skip[...], 0.0), axis=1, keepdims=True)
    pieces = []
    for h in range(2):
        response = acc[:, h * LANES : (h + 1) * LANES].reshape(S, SLAB, LANES)
        pieces.append(response + scale[None] * rx[...].astype(F32)[:, h * SLAB : (h + 1) * SLAB])
    sg[...] = jnp.concatenate(pieces, axis=1).astype(BF16)
    each(lambda k: response_copy(k).start())
    for k in range(group):
        twin_copy(k).start()
    rg[pl.ds(0, 1)] = sg[pl.ds(seq, 1)]

    pltpu.make_async_copy(wv.at[0], wv.at[0], w_local.at[0]).wait()

    def turn(side):
        for h in range(2):
            piece = gs[...].astype(F32)[:, h * SLAB : (h + 1) * SLAB].reshape(width, LANES)
            gated[side, h * LANES : (h + 1) * LANES, :] = piece.T.astype(BF16)

    for n in order:
        some_responses(n).wait_recv()
        for k in range(n * group, (n + 1) * group):
            s = (seq + k) % S
            slab = (sq[s].astype(F32) * rg[k].astype(F32)).astype(BF16)
            gk[k] = slab
            gs[s] = slab
        if n > 0:
            relay(n).start()
    for i in range(half // 2):
        direct(i).wait_recv()
        forward(i).start()
    turn(0)

    def chunk_of(i, parity):
        return (core + parity) % 2 * half + i // 2

    for i in range(CHUNKS):
        term = jnp.dot(gated[0], wv[0, chunk_of(i, i % 2)], preferred_element_type=F32)
        part[i] = term.reshape(Y, 2, rows // 2, chunk)
    remote(qx, qx, h_send.at[1], h_recv.at[1], across).wait()
    all_twins.wait_recv()
    for k in range(group):
        s = (seq + k) % S
        gs[s] = (qx[k].astype(F32) * hx[k].astype(F32)).astype(BF16)
    for n in order:
        if n > 0:
            relay(n).wait_recv()
    for k in range(group, S):
        gs[(seq + k) % S] = gx[k]
    turn(1)

    steps = [((Y - 1) // 2, Y // 2), (Y // 2, (Y - 1) // 2)]

    def hop(i, slot, target, device):
        return remote(ss.at[i, slot], sr.at[i, target], r_send.at[0], r_recv.at[i, target], device)

    def last_hop(i, slot, side, apart):
        half_rows = ss.at[i, slot, (xl + apart) % 2]
        return remote(
            half_rows, lr.at[i, side, apart], r_send.at[0], l_recv.at[i, side, apart], neighbours[side][apart]
        )

    def pairs(batch, function):
        def step(pair, _):
            for parity in range(2):
                function(2 * pair + parity, parity)
            return 0

        lax.fori_loop(batch * half // 2, (batch + 1) * half // 2, step, 0)

    def project(i, parity):
        j = chunk_of(i, parity)
        term = jnp.dot(gated[1], wv[1, j], preferred_element_type=F32)
        part[i] += term.reshape(Y, 2, rows // 2, chunk)
        fo[i] = part[i, y, 1 - xl].astype(BF16)
        remote(fo.at[i], fr.at[i], p_sem.at[0], p_sem.at[1], across).start()
        advance(0, i, parity)

    def advance(s, i, parity):
        up, low = steps[parity]
        for side, slot, first, count, owner in (
            (0, 0, 0, up, (y + up - s) % Y),
            (1, up, up - 1, low, (y + Y - low + s) % Y),
        ):
            if s >= count:
                continue
            total = part[i, owner]
            if s > 0:
                hop(i, slot + s - 1, first + s - 1, neighbours[side][0]).wait_recv()
                total = total + sr[i, first + s - 1].astype(F32)
            ss[i, slot + s] = total.astype(BF16)
            if s < count - 1:
                hop(i, slot + s, first + s, neighbours[side][0]).start()
            else:
                last_hop(i, slot + s, side, 0).start()
                last_hop(i, slot + s, side, 1).start()

    def finish(i, parity):
        j = chunk_of(i, parity)
        for apart in range(2):
            total = part[i, y, xl] if apart == 0 else fr[i].astype(F32)
            for side in range(2):
                last_hop(i, 0, side, apart).wait_recv()
                total = total + lr[i, side, apart].astype(F32)
            place = pl.ds(pl.multiple_of((xl + apart) % 2 * wide + j * chunk, LANES), chunk)
            result[:, place] = total.astype(BF16)
            pltpu.make_async_copy(result.at[:, place], out.at[:, place], o_sem.at[0]).start()

    for i in range(half):
        if i % 2 == 1:
            forwarded(i // 2).wait_recv()
        project(i, i % 2)
    all_taps.wait_send()
    all_signals.wait_send()
    all_responses.wait_send()
    all_relays.wait_send()
    all_twins.wait_send()
    for n in range(half // 2, half):
        direct(n).wait_recv()
        forward(n).start()
    pairs(0, functools.partial(advance, 1))
    for i in range(half, CHUNKS):
        if i % 2 == 1:
            forwarded(i // 2).wait_recv()
        project(i, i % 2)
    for s in range(2, Y // 2):
        pairs(0, functools.partial(advance, s))
        pairs(1, functools.partial(advance, s - 1))
    remote(fo, fr, p_sem.at[0], p_sem.at[1], across).wait()
    pairs(0, finish)
    if Y // 2 > 1:
        pairs(1, functools.partial(advance, Y // 2 - 1))
    pairs(1, finish)

    remote(wv.at[0, pl.ds(0, half)], wv.at[0, pl.ds(0, half)], wd_send.at[0], wd_recv.at[0], across).wait_send()
    remote(wv.at[1, pl.ds(0, half)], wv.at[1, pl.ds(0, half)], wf_send.at[0], wf_recv.at[0], beside).wait_send()
    remote(ss, ss, r_send.at[0], p_sem.at[1], ahead).wait_send()
    pltpu.make_async_copy(result, out, o_sem.at[0]).wait()


def body(query, key_branch, value, filters, skip, weight):
    S = lax.axis_size("seq")
    T = lax.axis_size("tensor")
    Y = T // 2
    width = query.shape[1]
    columns = weight.shape[1]
    chunk = columns // 2 // CHUNKS
    rows = BLOCK // Y
    dma = pltpu.SemaphoreType.DMA
    slab = pltpu.VMEM((S, 2 * SLAB, LANES), BF16)
    return pl.pallas_call(
        functools.partial(kernel, S, Y),
        out_shape=jax.ShapeDtypeStruct((BLOCK // T, columns), BF16),
        in_specs=[pl.BlockSpec(memory_space=pltpu.HBM)] * 6,
        out_specs=pl.BlockSpec(memory_space=pltpu.HBM),
        scratch_shapes=[
            pltpu.VMEM((3, *query.shape), BF16), pltpu.VMEM(filters.shape, F32), pltpu.VMEM((1, width), F32), dma((3,)),
            slab, slab, slab,
            pltpu.VMEM((filters.shape[0], 2, LANES), F32), pltpu.VMEM((S, 2, LANES), F32),
            pltpu.VMEM((S + 1, 2, LANES, BLOCK), BF16),
            pltpu.VMEM((S * SLAB, UNROLL * BLOCK), BF16),
            pltpu.VMEM((S * SLAB, BLOCK), F32),
            slab, slab, slab, slab, slab,
            pltpu.VMEM((S // GROUPS_OF_SLABS, 2 * SLAB, LANES), BF16), pltpu.VMEM((S // GROUPS_OF_SLABS, 2 * SLAB, LANES), BF16),
            pltpu.VMEM((2, BLOCK, width), BF16),
            pltpu.VMEM((2, CHUNKS, width, chunk), BF16),
            pltpu.VMEM((CHUNKS, Y, 2, rows // 2, chunk), F32),
            pltpu.VMEM((CHUNKS, Y - 1, 2, rows // 2, chunk), BF16),
            pltpu.VMEM((CHUNKS, Y - 3, 2, rows // 2, chunk), BF16),
            pltpu.VMEM((CHUNKS, 2, 2, rows // 2, chunk), BF16),
            pltpu.VMEM((CHUNKS, rows // 2, chunk), BF16),
            pltpu.VMEM((CHUNKS, rows // 2, chunk), BF16),
            pltpu.VMEM((BLOCK // T, columns), BF16),
            dma((1,)), dma((1,)), dma((1,)), dma((1,)), dma((1,)), dma((GROUPS_OF_SLABS,)),
            dma((1,)), dma((GROUPS_OF_SLABS,)), dma((2,)), dma((2,)),
            dma((1,)),
            dma((1,)), dma((CHUNKS // 2,)), dma((1,)), dma((CHUNKS // 2,)),
            dma((1,)), dma((CHUNKS, Y - 3)), dma((CHUNKS, 2, 2)), dma((2,)), dma((1,)),
        ],
        compiler_params=pltpu.CompilerParams(
            collective_id=0, has_side_effects=True, vmem_limit_bytes=60 * 2**20
        ),
        name="hyena",
    )(query, key_branch, value, filters, skip.reshape(1, width), weight)


def solution(mesh):
    return jax.shard_map(
        body,
        mesh=mesh,
        in_specs=(
            P("seq", "tensor"),
            P("seq", "tensor"),
            P("seq", "tensor"),
            P("tensor", "seq"),
            P("tensor"),
            P("tensor", None),
        ),
        out_specs=P(("seq", "tensor"), None),
        check_vma=False,
    )
```

```python
import functools

import jax
import jax.numpy as jnp
from jax import lax
from jax.experimental import pallas as pl
from jax.experimental.pallas import tpu as pltpu
from jax.sharding import PartitionSpec as P

F32 = jnp.float32
BF16 = jnp.bfloat16
LANES = 128
GROUPS_OF_SLABS = 4
SLAB = 8
BLOCK = 2 * LANES
UNROLL = 4
CHUNKS = 8


def remote(src, dst, send, recv, device):
    return pltpu.make_async_remote_copy(
        src_ref=src,
        dst_ref=dst,
        send_sem=send,
        recv_sem=recv,
        device_id=device,
        device_id_type=pl.DeviceIdType.MESH,
    )


def kernel(
    S, Y,
    query_in, key_in, value_in, filters_in, skip_in, weight, out,
    factors, filters, skip, i_sem,
    sx, rx, sq, sf, rf, toeplitz, lhs, acc, sg, rg, gk, gx, gs, qx, hx, gated, wv, part, ss, sr, lr, fo, fr,
    x_send, x_recv, f_send, f_recv, g_send, g_recv, e_send, e_recv, h_send, h_recv,
    w_local, wd_send, wd_recv, wf_send, wf_recv, r_send, r_recv, l_recv, p_sem,
):
    seq = lax.axis_index("seq")
    ten = lax.axis_index("tensor")
    y = ten // 2
    xl = ten % 2
    core = seq % 2
    across = (seq, ten + 1 - 2 * xl)
    around = (seq + 2 - 4 * (seq // 2 % 2), ten + 1 - 2 * xl)
    beside = (seq + 1 - 2 * core, ten)
    ahead = (seq, (ten + 2) % (2 * Y))
    behind = (seq, (ten + 2 * Y - 2) % (2 * Y))
    neighbours = ((ahead, (seq, (ten + 3 - 2 * xl) % (2 * Y))), (behind, (seq, (ten + 2 * Y - 1 - 2 * xl) % (2 * Y))))
    width = factors.shape[2]
    columns = weight.shape[1]
    wide = columns // 2
    chunk = wide // CHUNKS
    half = CHUNKS // 2
    rows = BLOCK // Y
    group = S // GROUPS_OF_SLABS

    inputs = [
        pltpu.make_async_copy(key_in, factors.at[0], i_sem.at[0]),
        pltpu.make_async_copy(value_in, factors.at[1], i_sem.at[0]),
        pltpu.make_async_copy(query_in, factors.at[2], i_sem.at[0]),
        pltpu.make_async_copy(filters_in, filters, i_sem.at[1]),
        pltpu.make_async_copy(skip_in, skip, i_sem.at[2]),
    ]
    for copy in inputs:
        copy.start()

    barrier = pltpu.get_barrier_semaphore()

    def greet(device):
        pl.semaphore_signal(barrier, inc=1, device_id=device, device_id_type=pl.DeviceIdType.MESH)

    for device in (across, around, *neighbours[0], *neighbours[1]):
        greet(device)

    def greet_seq(d, _):
        greet(((seq + d) % S, ten))
        return 0

    lax.fori_loop(1, S, greet_seq, 0, unroll=True)
    for k in range(1, group):
        greet(((seq + k) % S, ten + 1 - 2 * xl))

    def own_weight(j):
        return pltpu.make_async_copy(
            weight.at[:, pl.ds(pl.multiple_of(xl * wide + j * chunk, LANES), chunk)], wv.at[0, j], w_local.at[0]
        )

    for j in range(CHUNKS):
        own_weight(j).start()

    pltpu.make_async_copy(factors, factors, i_sem.at[0]).wait()
    inputs[3].wait()
    inputs[4].wait()

    def slabs(array):
        turned = array.T
        return jnp.concatenate(
            [turned[:, :LANES].reshape(S, SLAB, LANES), turned[:, LANES:].reshape(S, SLAB, LANES)], axis=1
        ).astype(BF16)

    sx[...] = slabs(factors[0].astype(F32) * factors[1].astype(F32))
    for g in range(filters.shape[0]):
        for h in range(2):
            sf[g, h : h + 1, :] = filters[g : g + 1, h * LANES : (h + 1) * LANES]
    rx[pl.ds(seq, 1)] = sx[pl.ds(seq, 1)]
    rf[pl.ds(seq, 1)] = sf[pl.ds(seq // 2, 1)]

    pl.semaphore_wait(barrier, S + 4 + group)

    def taps_copy(k):
        p = (seq + S - k) % S
        return remote(sf.at[p // 2], rf.at[seq], f_send.at[0], f_recv.at[0], (p, ten))

    def signal_copy(k):
        p = (seq + S - k) % S
        return remote(sx.at[p], rx.at[seq], x_send.at[0], x_recv.at[0], (p, ten))

    def response_copy(k):
        p = (seq + S - k) % S
        return remote(sg.at[p], rg.at[k], g_send.at[0], g_recv.at[k // group], (p, ten))

    def twin_copy(k):
        p = (seq + S - k) % S
        return remote(sg.at[p], hx.at[k], h_send.at[0], h_recv.at[0], (p, ten + 1 - 2 * xl))

    def relay(n):
        span = pl.ds(n * group, group)
        return remote(gk.at[span], gx.at[span], e_send.at[0], e_recv.at[n], across)

    order = [GROUPS_OF_SLABS // 2, GROUPS_OF_SLABS // 2 - 1] + list(range(GROUPS_OF_SLABS // 2 + 1, GROUPS_OF_SLABS)) + [0]

    def each_of(n, function):
        def step(k, _):
            function(k)
            return 0

        lax.fori_loop(max(n * group, 1), (n + 1) * group, step, 0)

    def each(function):
        for n in order:
            each_of(n, function)

    each(lambda k: taps_copy(k).start())
    each(lambda k: signal_copy(k).start())
    sq[...] = slabs(factors[2].astype(F32))
    for k in range(group):
        remote(sq.at[(seq + k) % S], qx.at[k], h_send.at[1], h_recv.at[1], across).start()

    def direct(i):
        j = core * half + i
        return remote(
            weight.at[:, pl.ds(pl.multiple_of((1 - xl) * wide + j * chunk, LANES), chunk)],
            wv.at[1, j], wd_send.at[0], wd_recv.at[i], across if i % 2 == 0 else around,
        )

    def forward(i):
        j = core * half + i
        return remote(wv.at[1, j], wv.at[1, j], wf_send.at[0], wf_recv.at[i], beside)

    def forwarded(i):
        j = (1 - core) * half + i
        return remote(wv.at[1, j], wv.at[1, j], wf_send.at[0], wf_recv.at[i], beside)

    for i in range(half):
        direct(i).start()

    everyone = pl.ds(0, S - 1)
    all_taps = remote(rf.at[everyone], rf.at[everyone], f_send.at[0], f_recv.at[0], across)
    all_signals = remote(rx.at[everyone], rx.at[everyone], x_send.at[0], x_recv.at[0], across)
    all_responses = remote(sg.at[everyone], rg.at[everyone], g_send.at[0], g_recv.at[0], across)
    far = pl.ds(group, S - group)
    all_relays = remote(gk.at[far], gx.at[far], e_send.at[0], e_recv.at[0], across)
    all_twins = remote(hx, hx, h_send.at[0], h_recv.at[0], across)

    def some_responses(n):
        span = pl.ds(0, group if n > 0 else group - 1)
        return remote(sg.at[span], rg.at[span], g_send.at[0], g_recv.at[n], across)

    all_taps.wait_recv()
    toeplitz[0, 1, :, 0:LANES] = jnp.zeros((LANES, LANES), BF16)
    lane = lax.broadcasted_iota(jnp.int32, (LANES, LANES), 1)
    down = lax.broadcasted_iota(jnp.int32, (LANES, LANES), 0)
    mask = lane >= down

    def build(a, before):
        for h in range(2):
            row = jnp.broadcast_to(rf[a, h : h + 1, :], (LANES, LANES))
            rolled = pltpu.roll(row, 0, 1, stride=1, stride_axis=0)
            block = jnp.where(mask, rolled, before).astype(BF16)
            before = rolled
            if h == 0:
                toeplitz[a, 0, :, 0:LANES] = block
                toeplitz[a, 1, :, LANES:BLOCK] = block
            else:
                toeplitz[a, 0, :, LANES:BLOCK] = block
                toeplitz[a + 1, 1, :, 0:LANES] = block
        return before

    lax.fori_loop(0, S, build, jnp.zeros((LANES, LANES), F32), unroll=4)

    all_signals.wait_recv()
    signal = rx[...].astype(F32)
    for h in range(2):
        piece = signal[:, h * SLAB : (h + 1) * SLAB, :].reshape(S * SLAB, LANES)
        for r in range(UNROLL):
            shifted = piece
            if r > 0:
                shifted = jnp.concatenate([jnp.zeros((r * SLAB, LANES), F32), piece[: (S - r) * SLAB]], axis=0)
            lhs[:, r * BLOCK + h * LANES : r * BLOCK + (h + 1) * LANES] = shifted.astype(BF16)
    for step in range(S // UNROLL):
        top = step * UNROLL * SLAB
        taps = toeplitz[step * UNROLL : (step + 1) * UNROLL].reshape(UNROLL * BLOCK, BLOCK)
        product = jnp.dot(lhs[: S * SLAB - top, :], taps, preferred_element_type=F32)
        if step == 0:
            acc[...] = product
        else:
            acc[top:, :] += product
    spot = lax.broadcasted_iota(jnp.int32, (SLAB, width), 1) - SLAB * seq
    picked = spot == lax.broadcasted_iota(jnp.int32, (SLAB, width), 0)
    scale = jnp.sum(jnp.where(picked, skip[...], 0.0), axis=1, keepdims=True)
    pieces = []
    for h in range(2):
        response = acc[:, h * LANES : (h + 1) * LANES].reshape(S, SLAB, LANES)
        pieces.append(response + scale[None] * rx[...].astype(F32)[:, h * SLAB : (h + 1) * SLAB])
    sg[...] = jnp.concatenate(pieces, axis=1).astype(BF16)
    each(lambda k: response_copy(k).start())
    for k in range(group):
        twin_copy(k).start()
    rg[pl.ds(0, 1)] = sg[pl.ds(seq, 1)]

    pltpu.make_async_copy(wv.at[0], wv.at[0], w_local.at[0]).wait()

    def turn(side):
        for h in range(2):
            piece = gs[...].astype(F32)[:, h * SLAB : (h + 1) * SLAB].reshape(width, LANES)
            gated[side, h * LANES : (h + 1) * LANES, :] = piece.T.astype(BF16)

    for n in order:
        some_responses(n).wait_recv()
        for k in range(n * group, (n + 1) * group):
            s = (seq + k) % S
            slab = (sq[s].astype(F32) * rg[k].astype(F32)).astype(BF16)
            gk[k] = slab
            gs[s] = slab
        if n > 0:
            relay(n).start()
    for i in range(half // 2):
        direct(i).wait_recv()
        forward(i).start()
    turn(0)

    def chunk_of(i, parity):
        return (core + parity) % 2 * half + i // 2

    for i in range(CHUNKS):
        term = jnp.dot(gated[0], wv[0, chunk_of(i, i % 2)], preferred_element_type=F32)
        part[i] = term.reshape(Y, 2, rows // 2, chunk)
    remote(qx, qx, h_send.at[1], h_recv.at[1], across).wait()
    all_twins.wait_recv()
    for k in range(group):
        s = (seq + k) % S
        gs[s] = (qx[k].astype(F32) * hx[k].astype(F32)).astype(BF16)
    for n in order:
        if n > 0:
            relay(n).wait_recv()
    for k in range(group, S):
        gs[(seq + k) % S] = gx[k]
    turn(1)

    steps = [((Y - 1) // 2, Y // 2), (Y // 2, (Y - 1) // 2)]

    def hop(i, slot, s, side):
        return remote(
            ss.at[i, slot], sr.at[i, s, side], r_send.at[0], r_recv.at[i, s], neighbours[side][0]
        )

    def last_hop(i, slot, side, apart):
        half_rows = ss.at[i, slot, (xl + apart) % 2]
        return remote(
            half_rows, lr.at[i, side, apart], r_send.at[0], l_recv.at[i], neighbours[side][apart]
        )

    def pairs(batch, function):
        def step(pair, _):
            for parity in range(2):
                function(2 * pair + parity, parity)
            return 0

        lax.fori_loop(batch * half // 2, (batch + 1) * half // 2, step, 0)

    def project(i, parity):
        j = chunk_of(i, parity)
        term = jnp.dot(gated[1], wv[1, j], preferred_element_type=F32)
        part[i] += term.reshape(Y, 2, rows // 2, chunk)
        fo[i] = part[i, y, 1 - xl].astype(BF16)
        remote(fo.at[i], fr.at[i], p_sem.at[0], p_sem.at[1], across).start()
        advance(0, i, parity)

    def advance(s, i, parity):
        up, low = steps[parity]
        if 0 < s < min(up, low):
            remote(sr.at[i, s - 1], sr.at[i, s - 1], r_send.at[0], r_recv.at[i, s - 1], ahead).wait_recv()
        elif 0 < s < max(up, low):
            hop(i, 0, s - 1, 0 if up > low else 1).wait_recv()
        for side, slot, count, owner in ((0, 0, up, (y + up - s) % Y), (1, up, low, (y + Y - low + s) % Y)):
            if s >= count:
                continue
            total = part[i, owner]
            if s > 0:
                total = total + sr[i, s - 1, side].astype(F32)
            ss[i, slot + s] = total.astype(BF16)
            if s < count - 1:
                hop(i, slot + s, s, side).start()
            else:
                last_hop(i, slot + s, side, 0).start()
                last_hop(i, slot + s, side, 1).start()

    def finish(i, parity):
        j = chunk_of(i, parity)
        remote(lr.at[i], lr.at[i], r_send.at[0], l_recv.at[i], ahead).wait_recv()
        for apart in range(2):
            total = part[i, y, xl] if apart == 0 else fr[i].astype(F32)
            for side in range(2):
                total = total + lr[i, side, apart].astype(F32)
            place = pl.ds(pl.multiple_of((xl + apart) % 2 * wide + j * chunk, LANES), chunk)
            out[:, place] = total.astype(BF16)

    for i in range(half):
        if i % 2 == 1:
            forwarded(i // 2).wait_recv()
        project(i, i % 2)
    all_taps.wait_send()
    all_signals.wait_send()
    all_responses.wait_send()
    all_relays.wait_send()
    all_twins.wait_send()
    for n in range(half // 2, half):
        direct(n).wait_recv()
        forward(n).start()
    last = Y // 2 - 1
    pairs(0, functools.partial(advance, 1))
    for i in range(half, CHUNKS):
        if i % 2 == 1:
            forwarded(i // 2).wait_recv()
        project(i, i % 2)
    for s in range(2, last):
        pairs(0, functools.partial(advance, s))
    for s in range(1, last):
        pairs(1, functools.partial(advance, s))
    pairs(0, functools.partial(advance, last))
    remote(fo, fr, p_sem.at[0], p_sem.at[1], across).wait()
    pairs(1, functools.partial(advance, last))
    pairs(0, finish)
    pairs(1, finish)

    remote(wv.at[0, pl.ds(0, half)], wv.at[0, pl.ds(0, half)], wd_send.at[0], wd_recv.at[0], across).wait_send()
    remote(wv.at[1, pl.ds(0, half)], wv.at[1, pl.ds(0, half)], wf_send.at[0], wf_recv.at[0], beside).wait_send()
    remote(ss, ss, r_send.at[0], p_sem.at[1], ahead).wait_send()


def body(query, key_branch, value, filters, skip, weight):
    S = lax.axis_size("seq")
    T = lax.axis_size("tensor")
    Y = T // 2
    width = query.shape[1]
    columns = weight.shape[1]
    chunk = columns // 2 // CHUNKS
    rows = BLOCK // Y
    dma = pltpu.SemaphoreType.DMA
    slab = pltpu.VMEM((S, 2 * SLAB, LANES), BF16)
    return pl.pallas_call(
        functools.partial(kernel, S, Y),
        out_shape=pltpu.VMEM((BLOCK // T, columns), BF16),
        in_specs=[pl.BlockSpec(memory_space=pltpu.HBM)] * 6,
        out_specs=pl.BlockSpec(memory_space=pltpu.VMEM),
        scratch_shapes=[
            pltpu.VMEM((3, *query.shape), BF16), pltpu.VMEM(filters.shape, F32), pltpu.VMEM((1, width), F32), dma((3,)),
            slab, slab, slab,
            pltpu.VMEM((filters.shape[0], 2, LANES), F32), pltpu.VMEM((S, 2, LANES), F32),
            pltpu.VMEM((S + 1, 2, LANES, BLOCK), BF16),
            pltpu.VMEM((S * SLAB, UNROLL * BLOCK), BF16),
            pltpu.VMEM((S * SLAB, BLOCK), F32),
            slab, slab, slab, slab, slab,
            pltpu.VMEM((S // GROUPS_OF_SLABS, 2 * SLAB, LANES), BF16), pltpu.VMEM((S // GROUPS_OF_SLABS, 2 * SLAB, LANES), BF16),
            pltpu.VMEM((2, BLOCK, width), BF16),
            pltpu.VMEM((2, CHUNKS, width, chunk), BF16),
            pltpu.VMEM((CHUNKS, Y, 2, rows // 2, chunk), F32),
            pltpu.VMEM((CHUNKS, Y - 1, 2, rows // 2, chunk), BF16),
            pltpu.VMEM((CHUNKS, Y // 2 - 1, 2, 2, rows // 2, chunk), BF16),
            pltpu.VMEM((CHUNKS, 2, 2, rows // 2, chunk), BF16),
            pltpu.VMEM((CHUNKS, rows // 2, chunk), BF16),
            pltpu.VMEM((CHUNKS, rows // 2, chunk), BF16),
            dma((1,)), dma((1,)), dma((1,)), dma((1,)), dma((1,)), dma((GROUPS_OF_SLABS,)),
            dma((1,)), dma((GROUPS_OF_SLABS,)), dma((2,)), dma((2,)),
            dma((1,)),
            dma((1,)), dma((CHUNKS // 2,)), dma((1,)), dma((CHUNKS // 2,)),
            dma((1,)), dma((CHUNKS, Y // 2 - 1)), dma((CHUNKS,)), dma((2,)),
        ],
        compiler_params=pltpu.CompilerParams(
            collective_id=0, has_side_effects=True, vmem_limit_bytes=60 * 2**20
        ),
        name="hyena",
    )(query, key_branch, value, filters, skip.reshape(1, width), weight)


def solution(mesh):
    return jax.shard_map(
        body,
        mesh=mesh,
        in_specs=(
            P("seq", "tensor"),
            P("seq", "tensor"),
            P("seq", "tensor"),
            P("tensor", "seq"),
            P("tensor"),
            P("tensor", None),
        ),
        out_specs=P(("seq", "tensor"), None),
        check_vma=False,
    )
```

```python
import functools

import jax
import jax.numpy as jnp
from jax import lax
from jax.experimental import pallas as pl
from jax.experimental.pallas import tpu as pltpu
from jax.sharding import PartitionSpec as P

F32 = jnp.float32
BF16 = jnp.bfloat16
LANES = 128
GROUPS_OF_SLABS = 4
SLAB = 8
BLOCK = 2 * LANES
UNROLL = 4
CHUNKS = 8


def remote(src, dst, send, recv, device):
    return pltpu.make_async_remote_copy(
        src_ref=src,
        dst_ref=dst,
        send_sem=send,
        recv_sem=recv,
        device_id=device,
        device_id_type=pl.DeviceIdType.MESH,
    )


def kernel(
    S, Y,
    query_in, key_in, value_in, filters_in, skip_in, weight, out,
    factors, filters, skip, i_sem,
    sx, rx, sq, sf, rf, toeplitz, lhs, acc, sg, rg, gk, gx, gs, qx, hx, gated, wv, part, ss, sr, lr, fo, fr,
    x_send, x_recv, f_send, f_recv, g_send, g_recv, e_send, e_recv, h_send, h_recv,
    w_local, wd_send, wd_recv, wf_send, wf_recv, r_send, r_recv, l_recv, p_sem,
):
    seq = lax.axis_index("seq")
    ten = lax.axis_index("tensor")
    y = ten // 2
    xl = ten % 2
    core = seq % 2
    across = (seq, ten + 1 - 2 * xl)
    around = (seq + 2 - 4 * (seq // 2 % 2), ten + 1 - 2 * xl)
    beside = (seq + 1 - 2 * core, ten)
    ahead = (seq, (ten + 2) % (2 * Y))
    behind = (seq, (ten + 2 * Y - 2) % (2 * Y))
    neighbours = ((ahead, (seq, (ten + 3 - 2 * xl) % (2 * Y))), (behind, (seq, (ten + 2 * Y - 1 - 2 * xl) % (2 * Y))))
    width = factors.shape[2]
    columns = weight.shape[1]
    wide = columns // 2
    chunk = wide // CHUNKS
    half = CHUNKS // 2
    rows = BLOCK // Y
    group = S // GROUPS_OF_SLABS

    inputs = [
        pltpu.make_async_copy(key_in, factors.at[0], i_sem.at[0]),
        pltpu.make_async_copy(value_in, factors.at[1], i_sem.at[0]),
        pltpu.make_async_copy(query_in, factors.at[2], i_sem.at[0]),
        pltpu.make_async_copy(filters_in, filters, i_sem.at[1]),
        pltpu.make_async_copy(skip_in, skip, i_sem.at[2]),
    ]
    for copy in inputs:
        copy.start()

    barrier = pltpu.get_barrier_semaphore()

    def greet(device):
        pl.semaphore_signal(barrier, inc=1, device_id=device, device_id_type=pl.DeviceIdType.MESH)

    for device in (across, around, *neighbours[0], *neighbours[1]):
        greet(device)

    def greet_seq(d, _):
        greet(((seq + d) % S, ten))
        return 0

    lax.fori_loop(1, S, greet_seq, 0, unroll=True)
    for k in range(1, group):
        greet(((seq + k) % S, ten + 1 - 2 * xl))

    def own_weight(j):
        return pltpu.make_async_copy(
            weight.at[:, pl.ds(pl.multiple_of(xl * wide + j * chunk, LANES), chunk)], wv.at[0, j], w_local.at[0]
        )

    for j in range(CHUNKS):
        own_weight(j).start()

    pltpu.make_async_copy(factors, factors, i_sem.at[0]).wait()
    inputs[3].wait()
    inputs[4].wait()

    def slabs(array):
        turned = array.T
        return jnp.concatenate(
            [turned[:, :LANES].reshape(S, SLAB, LANES), turned[:, LANES:].reshape(S, SLAB, LANES)], axis=1
        ).astype(BF16)

    sx[...] = slabs(factors[0].astype(F32) * factors[1].astype(F32))
    for g in range(filters.shape[0]):
        for h in range(2):
            sf[g, h : h + 1, :] = filters[g : g + 1, h * LANES : (h + 1) * LANES]
    rx[pl.ds(seq, 1)] = sx[pl.ds(seq, 1)]
    rf[pl.ds(seq, 1)] = sf[pl.ds(seq // 2, 1)]

    pl.semaphore_wait(barrier, S + 4 + group)

    def taps_copy(k):
        p = (seq + S - k) % S
        return remote(sf.at[p // 2], rf.at[seq], f_send.at[0], f_recv.at[0], (p, ten))

    def signal_copy(k):
        p = (seq + S - k) % S
        return remote(sx.at[p], rx.at[seq], x_send.at[0], x_recv.at[0], (p, ten))

    def response_copy(k):
        p = (seq + S - k) % S
        return remote(sg.at[p], rg.at[k], g_send.at[0], g_recv.at[k // group], (p, ten))

    def twin_copy(k):
        p = (seq + S - k) % S
        return remote(sg.at[p], hx.at[k], h_send.at[0], h_recv.at[0], (p, ten + 1 - 2 * xl))

    def relay(n):
        span = pl.ds(n * group, group)
        return remote(gk.at[span], gx.at[span], e_send.at[0], e_recv.at[n], across)

    order = [GROUPS_OF_SLABS // 2, GROUPS_OF_SLABS // 2 - 1] + list(range(GROUPS_OF_SLABS // 2 + 1, GROUPS_OF_SLABS)) + [0]

    def each(function):
        function(S // 2)

        def step(m, _):
            function(S // 2 - m)
            function(S // 2 + m)
            return 0

        lax.fori_loop(1, S // 2, step, 0, unroll=True)

    each(lambda k: taps_copy(k).start())
    each(lambda k: signal_copy(k).start())
    sq[...] = slabs(factors[2].astype(F32))
    for k in range(group):
        remote(sq.at[(seq + k) % S], qx.at[k], h_send.at[1], h_recv.at[1], across).start()

    def direct(i):
        j = core * half + i
        return remote(
            weight.at[:, pl.ds(pl.multiple_of((1 - xl) * wide + j * chunk, LANES), chunk)],
            wv.at[1, j], wd_send.at[0], wd_recv.at[i], across if i % 2 == 0 else around,
        )

    def forward(i):
        j = core * half + i
        return remote(wv.at[1, j], wv.at[1, j], wf_send.at[0], wf_recv.at[i], beside)

    def forwarded(i):
        j = (1 - core) * half + i
        return remote(wv.at[1, j], wv.at[1, j], wf_send.at[0], wf_recv.at[i], beside)

    for i in range(half):
        direct(i).start()

    everyone = pl.ds(0, S - 1)
    all_taps = remote(rf.at[everyone], rf.at[everyone], f_send.at[0], f_recv.at[0], across)
    all_signals = remote(rx.at[everyone], rx.at[everyone], x_send.at[0], x_recv.at[0], across)
    all_responses = remote(sg.at[everyone], rg.at[everyone], g_send.at[0], g_recv.at[0], across)
    far = pl.ds(group, S - group)
    all_relays = remote(gk.at[far], gx.at[far], e_send.at[0], e_recv.at[0], across)
    all_twins = remote(hx, hx, h_send.at[0], h_recv.at[0], across)

    def some_responses(n):
        span = pl.ds(0, group if n > 0 else group - 1)
        return remote(sg.at[span], rg.at[span], g_send.at[0], g_recv.at[n], across)

    all_taps.wait_recv()
    toeplitz[0, 1, :, 0:LANES] = jnp.zeros((LANES, LANES), BF16)
    lane = lax.broadcasted_iota(jnp.int32, (LANES, LANES), 1)
    down = lax.broadcasted_iota(jnp.int32, (LANES, LANES), 0)
    mask = lane >= down

    def build(a, before):
        for h in range(2):
            row = jnp.broadcast_to(rf[a, h : h + 1, :], (LANES, LANES))
            rolled = pltpu.roll(row, 0, 1, stride=1, stride_axis=0)
            block = jnp.where(mask, rolled, before).astype(BF16)
            before = rolled
            if h == 0:
                toeplitz[a, 0, :, 0:LANES] = block
                toeplitz[a, 1, :, LANES:BLOCK] = block
            else:
                toeplitz[a, 0, :, LANES:BLOCK] = block
                toeplitz[a + 1, 1, :, 0:LANES] = block
        return before

    lax.fori_loop(0, S, build, jnp.zeros((LANES, LANES), F32), unroll=4)

    all_signals.wait_recv()
    signal = rx[...].astype(F32)
    for h in range(2):
        piece = signal[:, h * SLAB : (h + 1) * SLAB, :].reshape(S * SLAB, LANES)
        for r in range(UNROLL):
            shifted = piece
            if r > 0:
                shifted = jnp.concatenate([jnp.zeros((r * SLAB, LANES), F32), piece[: (S - r) * SLAB]], axis=0)
            lhs[:, r * BLOCK + h * LANES : r * BLOCK + (h + 1) * LANES] = shifted.astype(BF16)
    for step in range(S // UNROLL):
        top = step * UNROLL * SLAB
        taps = toeplitz[step * UNROLL : (step + 1) * UNROLL].reshape(UNROLL * BLOCK, BLOCK)
        product = jnp.dot(lhs[: S * SLAB - top, :], taps, preferred_element_type=F32)
        if step == 0:
            acc[...] = product
        else:
            acc[top:, :] += product
    spot = lax.broadcasted_iota(jnp.int32, (SLAB, width), 1) - SLAB * seq
    picked = spot == lax.broadcasted_iota(jnp.int32, (SLAB, width), 0)
    scale = jnp.sum(jnp.where(picked, skip[...], 0.0), axis=1, keepdims=True)
    pieces = []
    for h in range(2):
        response = acc[:, h * LANES : (h + 1) * LANES].reshape(S, SLAB, LANES)
        pieces.append(response + scale[None] * rx[...].astype(F32)[:, h * SLAB : (h + 1) * SLAB])
    sg[...] = jnp.concatenate(pieces, axis=1).astype(BF16)
    each(lambda k: response_copy(k).start())
    for k in range(group):
        twin_copy(k).start()
    rg[pl.ds(0, 1)] = sg[pl.ds(seq, 1)]

    pltpu.make_async_copy(wv.at[0], wv.at[0], w_local.at[0]).wait()

    def turn(side):
        for h in range(2):
            piece = gs[...].astype(F32)[:, h * SLAB : (h + 1) * SLAB].reshape(width, LANES)
            gated[side, h * LANES : (h + 1) * LANES, :] = piece.T.astype(BF16)

    for n in order:
        some_responses(n).wait_recv()
        for k in range(n * group, (n + 1) * group):
            s = (seq + k) % S
            slab = (sq[s].astype(F32) * rg[k].astype(F32)).astype(BF16)
            gk[k] = slab
            gs[s] = slab
        if n > 0:
            relay(n).start()
    for i in range(half // 2):
        direct(i).wait_recv()
        forward(i).start()
    turn(0)

    def chunk_of(i, parity):
        return (core + parity) % 2 * half + i // 2

    for i in range(CHUNKS):
        term = jnp.dot(gated[0], wv[0, chunk_of(i, i % 2)], preferred_element_type=F32)
        part[i] = term.reshape(Y, 2, rows // 2, chunk)
    remote(qx, qx, h_send.at[1], h_recv.at[1], across).wait()
    all_twins.wait_recv()
    for k in range(group):
        s = (seq + k) % S
        gs[s] = (qx[k].astype(F32) * hx[k].astype(F32)).astype(BF16)
    for n in order:
        if n > 0:
            relay(n).wait_recv()
    for k in range(group, S):
        gs[(seq + k) % S] = gx[k]
    turn(1)

    steps = [((Y - 1) // 2, Y // 2), (Y // 2, (Y - 1) // 2)]

    def hop(i, slot, s, side):
        return remote(
            ss.at[i, slot], sr.at[i, s, side], r_send.at[0], r_recv.at[i, s], neighbours[side][0]
        )

    def last_hop(i, slot, side, apart):
        half_rows = ss.at[i, slot, (xl + apart) % 2]
        return remote(
            half_rows, lr.at[i, side, apart], r_send.at[0], l_recv.at[i], neighbours[side][apart]
        )

    def pairs(batch, function):
        def step(pair, _):
            for parity in range(2):
                function(2 * pair + parity, parity)
            return 0

        lax.fori_loop(batch * half // 2, (batch + 1) * half // 2, step, 0)

    def project(i, parity):
        j = chunk_of(i, parity)
        term = jnp.dot(gated[1], wv[1, j], preferred_element_type=F32)
        part[i] += term.reshape(Y, 2, rows // 2, chunk)
        fo[i] = part[i, y, 1 - xl].astype(BF16)
        remote(fo.at[i], fr.at[i], p_sem.at[0], p_sem.at[1], across).start()
        advance(0, i, parity)

    def advance(s, i, parity):
        up, low = steps[parity]
        if 0 < s < min(up, low):
            remote(sr.at[i, s - 1], sr.at[i, s - 1], r_send.at[0], r_recv.at[i, s - 1], ahead).wait_recv()
        elif 0 < s < max(up, low):
            hop(i, 0, s - 1, 0 if up > low else 1).wait_recv()
        for side, slot, count, owner in ((0, 0, up, (y + up - s) % Y), (1, up, low, (y + Y - low + s) % Y)):
            if s >= count:
                continue
            total = part[i, owner]
            if s > 0:
                total = total + sr[i, s - 1, side].astype(F32)
            ss[i, slot + s] = total.astype(BF16)
            if s < count - 1:
                hop(i, slot + s, s, side).start()
            else:
                last_hop(i, slot + s, side, 0).start()
                last_hop(i, slot + s, side, 1).start()

    def finish(i, parity):
        j = chunk_of(i, parity)
        remote(lr.at[i], lr.at[i], r_send.at[0], l_recv.at[i], ahead).wait_recv()
        for apart in range(2):
            total = part[i, y, xl] if apart == 0 else fr[i].astype(F32)
            for side in range(2):
                total = total + lr[i, side, apart].astype(F32)
            place = pl.ds(pl.multiple_of((xl + apart) % 2 * wide + j * chunk, LANES), chunk)
            out[:, place] = total.astype(BF16)

    for i in range(half):
        if i % 2 == 1:
            forwarded(i // 2).wait_recv()
        project(i, i % 2)
    all_taps.wait_send()
    all_signals.wait_send()
    all_responses.wait_send()
    all_relays.wait_send()
    all_twins.wait_send()
    for n in range(half // 2, half):
        direct(n).wait_recv()
        forward(n).start()
    last = Y // 2 - 1
    pairs(0, functools.partial(advance, 1))
    for i in range(half, CHUNKS):
        if i % 2 == 1:
            forwarded(i // 2).wait_recv()
        project(i, i % 2)
    for s in range(2, last):
        pairs(0, functools.partial(advance, s))
    for s in range(1, last):
        pairs(1, functools.partial(advance, s))
    pairs(0, functools.partial(advance, last))
    remote(fo, fr, p_sem.at[0], p_sem.at[1], across).wait()
    pairs(1, functools.partial(advance, last))
    pairs(0, finish)
    pairs(1, finish)

    remote(wv.at[0, pl.ds(0, half)], wv.at[0, pl.ds(0, half)], wd_send.at[0], wd_recv.at[0], across).wait_send()
    remote(wv.at[1, pl.ds(0, half)], wv.at[1, pl.ds(0, half)], wf_send.at[0], wf_recv.at[0], beside).wait_send()
    remote(ss, ss, r_send.at[0], p_sem.at[1], ahead).wait_send()


def body(query, key_branch, value, filters, skip, weight):
    S = lax.axis_size("seq")
    T = lax.axis_size("tensor")
    Y = T // 2
    width = query.shape[1]
    columns = weight.shape[1]
    chunk = columns // 2 // CHUNKS
    rows = BLOCK // Y
    dma = pltpu.SemaphoreType.DMA
    slab = pltpu.VMEM((S, 2 * SLAB, LANES), BF16)
    return pl.pallas_call(
        functools.partial(kernel, S, Y),
        out_shape=pltpu.VMEM((BLOCK // T, columns), BF16),
        in_specs=[pl.BlockSpec(memory_space=pltpu.HBM)] * 6,
        out_specs=pl.BlockSpec(memory_space=pltpu.VMEM),
        scratch_shapes=[
            pltpu.VMEM((3, *query.shape), BF16), pltpu.VMEM(filters.shape, F32), pltpu.VMEM((1, width), F32), dma((3,)),
            slab, slab, slab,
            pltpu.VMEM((filters.shape[0], 2, LANES), F32), pltpu.VMEM((S, 2, LANES), F32),
            pltpu.VMEM((S + 1, 2, LANES, BLOCK), BF16),
            pltpu.VMEM((S * SLAB, UNROLL * BLOCK), BF16),
            pltpu.VMEM((S * SLAB, BLOCK), F32),
            slab, slab, slab, slab, slab,
            pltpu.VMEM((S // GROUPS_OF_SLABS, 2 * SLAB, LANES), BF16), pltpu.VMEM((S // GROUPS_OF_SLABS, 2 * SLAB, LANES), BF16),
            pltpu.VMEM((2, BLOCK, width), BF16),
            pltpu.VMEM((2, CHUNKS, width, chunk), BF16),
            pltpu.VMEM((CHUNKS, Y, 2, rows // 2, chunk), F32),
            pltpu.VMEM((CHUNKS, Y - 1, 2, rows // 2, chunk), BF16),
            pltpu.VMEM((CHUNKS, Y // 2 - 1, 2, 2, rows // 2, chunk), BF16),
            pltpu.VMEM((CHUNKS, 2, 2, rows // 2, chunk), BF16),
            pltpu.VMEM((CHUNKS, rows // 2, chunk), BF16),
            pltpu.VMEM((CHUNKS, rows // 2, chunk), BF16),
            dma((1,)), dma((1,)), dma((1,)), dma((1,)), dma((1,)), dma((GROUPS_OF_SLABS,)),
            dma((1,)), dma((GROUPS_OF_SLABS,)), dma((2,)), dma((2,)),
            dma((1,)),
            dma((1,)), dma((CHUNKS // 2,)), dma((1,)), dma((CHUNKS // 2,)),
            dma((1,)), dma((CHUNKS, Y // 2 - 1)), dma((CHUNKS,)), dma((2,)),
        ],
        compiler_params=pltpu.CompilerParams(
            collective_id=0, has_side_effects=True, vmem_limit_bytes=60 * 2**20
        ),
        name="hyena",
    )(query, key_branch, value, filters, skip.reshape(1, width), weight)


def solution(mesh):
    return jax.shard_map(
        body,
        mesh=mesh,
        in_specs=(
            P("seq", "tensor"),
            P("seq", "tensor"),
            P("seq", "tensor"),
            P("tensor", "seq"),
            P("tensor"),
            P("tensor", None),
        ),
        out_specs=P(("seq", "tensor"), None),
        check_vma=False,
    )
```

```python
import functools

import jax
import jax.numpy as jnp
from jax import lax
from jax.experimental import pallas as pl
from jax.experimental.pallas import tpu as pltpu
from jax.sharding import PartitionSpec as P

F32 = jnp.float32
BF16 = jnp.bfloat16
LANES = 128
GROUPS_OF_SLABS = 8
SLAB = 8
BLOCK = 2 * LANES
UNROLL = 4
CHUNKS = 8


def remote(src, dst, send, recv, device):
    return pltpu.make_async_remote_copy(
        src_ref=src,
        dst_ref=dst,
        send_sem=send,
        recv_sem=recv,
        device_id=device,
        device_id_type=pl.DeviceIdType.MESH,
    )


def kernel(
    S, Y,
    query_in, key_in, value_in, filters_in, skip_in, weight, out,
    factors, filters, skip, i_sem,
    sx, rx, sq, sf, rf, toeplitz, lhs, acc, sg, rg, gk, gx, gs, qx, hx, gated, wv, part, ss, sr, lr, fo, fr,
    x_send, x_recv, f_send, f_recv, g_send, g_recv, e_send, e_recv, h_send, h_recv,
    w_local, wd_send, wd_recv, wf_send, wf_recv, r_send, r_recv, l_recv, p_sem,
):
    seq = lax.axis_index("seq")
    ten = lax.axis_index("tensor")
    y = ten // 2
    xl = ten % 2
    core = seq % 2
    across = (seq, ten + 1 - 2 * xl)
    around = (seq + 2 - 4 * (seq // 2 % 2), ten + 1 - 2 * xl)
    beside = (seq + 1 - 2 * core, ten)
    ahead = (seq, (ten + 2) % (2 * Y))
    behind = (seq, (ten + 2 * Y - 2) % (2 * Y))
    neighbours = ((ahead, (seq, (ten + 3 - 2 * xl) % (2 * Y))), (behind, (seq, (ten + 2 * Y - 1 - 2 * xl) % (2 * Y))))
    width = factors.shape[2]
    columns = weight.shape[1]
    wide = columns // 2
    chunk = wide // CHUNKS
    half = CHUNKS // 2
    rows = BLOCK // Y
    group = S // GROUPS_OF_SLABS
    near = range(-group, 2 * group)

    inputs = [
        pltpu.make_async_copy(key_in, factors.at[0], i_sem.at[0]),
        pltpu.make_async_copy(value_in, factors.at[1], i_sem.at[0]),
        pltpu.make_async_copy(query_in, factors.at[2], i_sem.at[0]),
        pltpu.make_async_copy(filters_in, filters, i_sem.at[1]),
        pltpu.make_async_copy(skip_in, skip, i_sem.at[2]),
    ]
    for copy in inputs:
        copy.start()

    barrier = pltpu.get_barrier_semaphore()

    def greet(device):
        pl.semaphore_signal(barrier, inc=1, device_id=device, device_id_type=pl.DeviceIdType.MESH)

    for device in (across, around, *neighbours[0], *neighbours[1]):
        greet(device)

    def greet_seq(d, _):
        greet(((seq + d) % S, ten))
        return 0

    lax.fori_loop(1, S, greet_seq, 0, unroll=True)
    for k in near:
        if k != 0:
            greet(((seq + S + k) % S, ten + 1 - 2 * xl))

    def own_weight(j):
        return pltpu.make_async_copy(
            weight.at[:, pl.ds(pl.multiple_of(xl * wide + j * chunk, LANES), chunk)], wv.at[0, j], w_local.at[0]
        )

    for j in range(CHUNKS):
        own_weight(j).start()

    pltpu.make_async_copy(factors, factors, i_sem.at[0]).wait()
    inputs[3].wait()
    inputs[4].wait()

    def slabs(array):
        turned = array.T
        return jnp.concatenate(
            [turned[:, :LANES].reshape(S, SLAB, LANES), turned[:, LANES:].reshape(S, SLAB, LANES)], axis=1
        ).astype(BF16)

    sx[...] = slabs(factors[0].astype(F32) * factors[1].astype(F32))
    for g in range(filters.shape[0]):
        for h in range(2):
            sf[g, h : h + 1, :] = filters[g : g + 1, h * LANES : (h + 1) * LANES]
    rx[pl.ds(seq, 1)] = sx[pl.ds(seq, 1)]
    rf[pl.ds(seq, 1)] = sf[pl.ds(seq // 2, 1)]

    pl.semaphore_wait(barrier, S + 4 + 3 * group)

    def taps_copy(k):
        p = (seq + S - k) % S
        return remote(sf.at[p // 2], rf.at[seq], f_send.at[0], f_recv.at[0], (p, ten))

    def signal_copy(k):
        p = (seq + S - k) % S
        return remote(sx.at[p], rx.at[seq], x_send.at[0], x_recv.at[0], (p, ten))

    def response_copy(k):
        p = (seq + S - k) % S
        return remote(sg.at[p], rg.at[k], g_send.at[0], g_recv.at[k // group], (p, ten))

    def twin_copy(k):
        p = (seq + S - k) % S
        return remote(sg.at[p], hx.at[k + group], h_send.at[0], h_recv.at[0], (p, ten + 1 - 2 * xl))

    def relay(n):
        span = pl.ds(n * group, group)
        return remote(gk.at[span], gx.at[span], e_send.at[0], e_recv.at[n], across)

    middle = GROUPS_OF_SLABS // 2
    order = [middle]
    for n in range(1, middle):
        order += [middle - n, middle + n]
    order += [0]
    far = order[:-3]

    def each(function):
        function(S // 2)

        def step(m, _):
            function(S // 2 - m)
            function(S // 2 + m)
            return 0

        lax.fori_loop(1, S // 2, step, 0, unroll=True)

    each(lambda k: taps_copy(k).start())
    each(lambda k: signal_copy(k).start())
    sq[...] = slabs(factors[2].astype(F32))
    for k in near:
        remote(sq.at[(seq + S + k) % S], qx.at[k + group], h_send.at[1], h_recv.at[1], across).start()

    def direct(i):
        j = core * half + i
        return remote(
            weight.at[:, pl.ds(pl.multiple_of((1 - xl) * wide + j * chunk, LANES), chunk)],
            wv.at[1, j], wd_send.at[0], wd_recv.at[i], across if i % 2 == 0 else around,
        )

    def forward(i):
        j = core * half + i
        return remote(wv.at[1, j], wv.at[1, j], wf_send.at[0], wf_recv.at[i], beside)

    def forwarded(i):
        j = (1 - core) * half + i
        return remote(wv.at[1, j], wv.at[1, j], wf_send.at[0], wf_recv.at[i], beside)

    def direct_part(i, part_of):
        j = core * half + i
        span = pl.ds(part_of * (width // 2), width // 2)
        place = pl.ds(pl.multiple_of((1 - xl) * wide + j * chunk, LANES), chunk)
        return remote(
            weight.at[span, place], wv.at[1, j, span], wd_send.at[0], wd_recv.at[i], across if i % 2 == 0 else around
        )

    for i in range(half // 2):
        direct(i).start()
    for i in range(half // 2, half):
        direct_part(i, 0).start()

    everyone = pl.ds(0, S - 1)
    all_taps = remote(rf.at[everyone], rf.at[everyone], f_send.at[0], f_recv.at[0], across)
    all_signals = remote(rx.at[everyone], rx.at[everyone], x_send.at[0], x_recv.at[0], across)
    all_responses = remote(sg.at[everyone], rg.at[everyone], g_send.at[0], g_recv.at[0], across)
    relayed = pl.ds(2 * group, S - 3 * group)
    all_relays = remote(gk.at[relayed], gx.at[relayed], e_send.at[0], e_recv.at[0], across)
    all_twins = remote(hx, hx, h_send.at[0], h_recv.at[0], across)

    def some_responses(n):
        span = pl.ds(0, group if n > 0 else group - 1)
        return remote(sg.at[span], rg.at[span], g_send.at[0], g_recv.at[n], across)

    all_taps.wait_recv()
    toeplitz[0, 1, :, 0:LANES] = jnp.zeros((LANES, LANES), BF16)
    lane = lax.broadcasted_iota(jnp.int32, (LANES, LANES), 1)
    down = lax.broadcasted_iota(jnp.int32, (LANES, LANES), 0)
    mask = lane >= down

    def build(a, before):
        for h in range(2):
            row = jnp.broadcast_to(rf[a, h : h + 1, :], (LANES, LANES))
            rolled = pltpu.roll(row, 0, 1, stride=1, stride_axis=0)
            block = jnp.where(mask, rolled, before).astype(BF16)
            before = rolled
            if h == 0:
                toeplitz[a, 0, :, 0:LANES] = block
                toeplitz[a, 1, :, LANES:BLOCK] = block
            else:
                toeplitz[a, 0, :, LANES:BLOCK] = block
                toeplitz[a + 1, 1, :, 0:LANES] = block
        return before

    lax.fori_loop(0, S, build, jnp.zeros((LANES, LANES), F32), unroll=4)

    all_signals.wait_recv()
    signal = rx[...].astype(F32)
    for h in range(2):
        piece = signal[:, h * SLAB : (h + 1) * SLAB, :].reshape(S * SLAB, LANES)
        for r in range(UNROLL):
            shifted = piece
            if r > 0:
                shifted = jnp.concatenate([jnp.zeros((r * SLAB, LANES), F32), piece[: (S - r) * SLAB]], axis=0)
            lhs[:, r * BLOCK + h * LANES : r * BLOCK + (h + 1) * LANES] = shifted.astype(BF16)
    for step in range(S // UNROLL):
        top = step * UNROLL * SLAB
        taps = toeplitz[step * UNROLL : (step + 1) * UNROLL].reshape(UNROLL * BLOCK, BLOCK)
        product = jnp.dot(lhs[: S * SLAB - top, :], taps, preferred_element_type=F32)
        if step == 0:
            acc[...] = product
        else:
            acc[top:, :] += product
    spot = lax.broadcasted_iota(jnp.int32, (SLAB, width), 1) - SLAB * seq
    picked = spot == lax.broadcasted_iota(jnp.int32, (SLAB, width), 0)
    scale = jnp.sum(jnp.where(picked, skip[...], 0.0), axis=1, keepdims=True)
    pieces = []
    for h in range(2):
        response = acc[:, h * LANES : (h + 1) * LANES].reshape(S, SLAB, LANES)
        pieces.append(response + scale[None] * rx[...].astype(F32)[:, h * SLAB : (h + 1) * SLAB])
    sg[...] = jnp.concatenate(pieces, axis=1).astype(BF16)
    each(lambda k: response_copy(k).start())
    for k in reversed(near):
        twin_copy(k).start()
    for i in range(half // 2, half):
        direct_part(i, 1).start()
    rg[pl.ds(0, 1)] = sg[pl.ds(seq, 1)]

    pltpu.make_async_copy(wv.at[0], wv.at[0], w_local.at[0]).wait()

    def turn(side):
        for h in range(2):
            piece = gs[...].astype(F32)[:, h * SLAB : (h + 1) * SLAB].reshape(width, LANES)
            gated[side, h * LANES : (h + 1) * LANES, :] = piece.T.astype(BF16)

    for n in order:
        some_responses(n).wait_recv()
        for k in range(n * group, (n + 1) * group):
            s = (seq + k) % S
            slab = (sq[s].astype(F32) * rg[k].astype(F32)).astype(BF16)
            gk[k] = slab
            gs[s] = slab
        if n in far:
            relay(n).start()
    for i in range(half // 2):
        direct(i).wait_recv()
        forward(i).start()
    turn(0)

    def chunk_of(i, parity):
        return (core + parity) % 2 * half + i // 2

    for i in range(CHUNKS):
        term = jnp.dot(gated[0], wv[0, chunk_of(i, i % 2)], preferred_element_type=F32)
        part[i] = term.reshape(Y, 2, rows // 2, chunk)
    remote(qx, qx, h_send.at[1], h_recv.at[1], across).wait()
    all_twins.wait_recv()
    for k in near:
        gs[(seq + S + k) % S] = (qx[k + group].astype(F32) * hx[k + group].astype(F32)).astype(BF16)
    for n in far:
        relay(n).wait_recv()
    for k in range(2 * group, S - group):
        gs[(seq + k) % S] = gx[k]
    turn(1)

    steps = [((Y - 1) // 2, Y // 2), (Y // 2, (Y - 1) // 2)]

    def hop(i, slot, s, side):
        return remote(
            ss.at[i, slot], sr.at[i, s, side], r_send.at[0], r_recv.at[i, s], neighbours[side][0]
        )

    def last_hop(i, slot, side, apart):
        half_rows = ss.at[i, slot, (xl + apart) % 2]
        return remote(
            half_rows, lr.at[i, side, apart], r_send.at[0], l_recv.at[i], neighbours[side][apart]
        )

    def pairs(batch, function):
        def step(pair, _):
            for parity in range(2):
                function(2 * pair + parity, parity)
            return 0

        lax.fori_loop(batch * half // 2, (batch + 1) * half // 2, step, 0)

    def project(i, parity):
        j = chunk_of(i, parity)
        term = jnp.dot(gated[1], wv[1, j], preferred_element_type=F32)
        part[i] += term.reshape(Y, 2, rows // 2, chunk)
        fo[i] = part[i, y, 1 - xl].astype(BF16)
        remote(fo.at[i], fr.at[i], p_sem.at[0], p_sem.at[1], across).start()
        advance(0, i, parity)

    def advance(s, i, parity):
        up, low = steps[parity]
        if 0 < s < min(up, low):
            remote(sr.at[i, s - 1], sr.at[i, s - 1], r_send.at[0], r_recv.at[i, s - 1], ahead).wait_recv()
        elif 0 < s < max(up, low):
            hop(i, 0, s - 1, 0 if up > low else 1).wait_recv()
        for side, slot, count, owner in ((0, 0, up, (y + up - s) % Y), (1, up, low, (y + Y - low + s) % Y)):
            if s >= count:
                continue
            total = part[i, owner]
            if s > 0:
                total = total + sr[i, s - 1, side].astype(F32)
            ss[i, slot + s] = total.astype(BF16)
            if s < count - 1:
                hop(i, slot + s, s, side).start()
            else:
                last_hop(i, slot + s, side, 0).start()
                last_hop(i, slot + s, side, 1).start()

    def finish(i, parity):
        j = chunk_of(i, parity)
        remote(lr.at[i], lr.at[i], r_send.at[0], l_recv.at[i], ahead).wait_recv()
        for apart in range(2):
            total = part[i, y, xl] if apart == 0 else fr[i].astype(F32)
            for side in range(2):
                total = total + lr[i, side, apart].astype(F32)
            place = pl.ds(pl.multiple_of((xl + apart) % 2 * wide + j * chunk, LANES), chunk)
            out[:, place] = total.astype(BF16)

    for i in range(half):
        if i % 2 == 1:
            forwarded(i // 2).wait_recv()
        project(i, i % 2)
    all_taps.wait_send()
    all_signals.wait_send()
    all_responses.wait_send()
    all_relays.wait_send()
    all_twins.wait_send()
    for n in range(half // 2, half):
        direct(n).wait_recv()
        forward(n).start()
    last = Y // 2 - 1
    pairs(0, functools.partial(advance, 1))
    for i in range(half, CHUNKS):
        if i % 2 == 1:
            forwarded(i // 2).wait_recv()
        project(i, i % 2)
    for s in range(2, last):
        pairs(0, functools.partial(advance, s))
    for s in range(1, last):
        pairs(1, functools.partial(advance, s))
    pairs(0, functools.partial(advance, last))
    remote(fo, fr, p_sem.at[0], p_sem.at[1], across).wait()
    pairs(1, functools.partial(advance, last))
    pairs(0, finish)
    pairs(1, finish)

    remote(wv.at[0, pl.ds(0, half)], wv.at[0, pl.ds(0, half)], wd_send.at[0], wd_recv.at[0], across).wait_send()
    remote(wv.at[1, pl.ds(0, half)], wv.at[1, pl.ds(0, half)], wf_send.at[0], wf_recv.at[0], beside).wait_send()
    remote(ss, ss, r_send.at[0], p_sem.at[1], ahead).wait_send()


def body(query, key_branch, value, filters, skip, weight):
    S = lax.axis_size("seq")
    T = lax.axis_size("tensor")
    Y = T // 2
    width = query.shape[1]
    columns = weight.shape[1]
    chunk = columns // 2 // CHUNKS
    rows = BLOCK // Y
    dma = pltpu.SemaphoreType.DMA
    slab = pltpu.VMEM((S, 2 * SLAB, LANES), BF16)
    return pl.pallas_call(
        functools.partial(kernel, S, Y),
        out_shape=pltpu.VMEM((BLOCK // T, columns), BF16),
        in_specs=[pl.BlockSpec(memory_space=pltpu.HBM)] * 6,
        out_specs=pl.BlockSpec(memory_space=pltpu.VMEM),
        scratch_shapes=[
            pltpu.VMEM((3, *query.shape), BF16), pltpu.VMEM(filters.shape, F32), pltpu.VMEM((1, width), F32), dma((3,)),
            slab, slab, slab,
            pltpu.VMEM((filters.shape[0], 2, LANES), F32), pltpu.VMEM((S, 2, LANES), F32),
            pltpu.VMEM((S + 1, 2, LANES, BLOCK), BF16),
            pltpu.VMEM((S * SLAB, UNROLL * BLOCK), BF16),
            pltpu.VMEM((S * SLAB, BLOCK), F32),
            slab, slab, slab, slab, slab,
            pltpu.VMEM((3 * S // GROUPS_OF_SLABS, 2 * SLAB, LANES), BF16),
            pltpu.VMEM((3 * S // GROUPS_OF_SLABS, 2 * SLAB, LANES), BF16),
            pltpu.VMEM((2, BLOCK, width), BF16),
            pltpu.VMEM((2, CHUNKS, width, chunk), BF16),
            pltpu.VMEM((CHUNKS, Y, 2, rows // 2, chunk), F32),
            pltpu.VMEM((CHUNKS, Y - 1, 2, rows // 2, chunk), BF16),
            pltpu.VMEM((CHUNKS, Y // 2 - 1, 2, 2, rows // 2, chunk), BF16),
            pltpu.VMEM((CHUNKS, 2, 2, rows // 2, chunk), BF16),
            pltpu.VMEM((CHUNKS, rows // 2, chunk), BF16),
            pltpu.VMEM((CHUNKS, rows // 2, chunk), BF16),
            dma((1,)), dma((1,)), dma((1,)), dma((1,)), dma((1,)), dma((GROUPS_OF_SLABS,)),
            dma((1,)), dma((GROUPS_OF_SLABS,)), dma((2,)), dma((2,)),
            dma((1,)),
            dma((1,)), dma((CHUNKS // 2,)), dma((1,)), dma((CHUNKS // 2,)),
            dma((1,)), dma((CHUNKS, Y // 2 - 1)), dma((CHUNKS,)), dma((2,)),
        ],
        compiler_params=pltpu.CompilerParams(
            collective_id=0, has_side_effects=True, vmem_limit_bytes=60 * 2**20
        ),
        name="hyena",
    )(query, key_branch, value, filters, skip.reshape(1, width), weight)


def solution(mesh):
    return jax.shard_map(
        body,
        mesh=mesh,
        in_specs=(
            P("seq", "tensor"),
            P("seq", "tensor"),
            P("seq", "tensor"),
            P("tensor", "seq"),
            P("tensor"),
            P("tensor", None),
        ),
        out_specs=P(("seq", "tensor"), None),
        check_vma=False,
    )
```

```python
import functools

import jax
import jax.numpy as jnp
from jax import lax
from jax.experimental import pallas as pl
from jax.experimental.pallas import tpu as pltpu
from jax.sharding import PartitionSpec as P

F32 = jnp.float32
BF16 = jnp.bfloat16
LANES = 128
GROUPS_OF_SLABS = 8
SLAB = 8
BLOCK = 2 * LANES
UNROLL = 4
CHUNKS = 8


def remote(src, dst, send, recv, device):
    return pltpu.make_async_remote_copy(
        src_ref=src,
        dst_ref=dst,
        send_sem=send,
        recv_sem=recv,
        device_id=device,
        device_id_type=pl.DeviceIdType.MESH,
    )


def kernel(
    S, Y,
    query_in, key_in, value_in, filters_in, skip_in, weight, out,
    factors, filters, skip, i_sem,
    sx, rx, sq, sf, rf, toeplitz, lhs, acc, sg, rg, gk, gx, gs, qx, hx, gated, wv, part, ss, sr, lr, fo, fr,
    x_send, x_recv, f_send, f_recv, g_send, g_recv, e_send, e_recv, h_send, h_recv,
    w_local, wd_send, wd_recv, wf_send, wf_recv, r_send, r_recv, l_recv, p_sem,
):
    seq = lax.axis_index("seq")
    ten = lax.axis_index("tensor")
    y = ten // 2
    xl = ten % 2
    core = seq % 2
    across = (seq, ten + 1 - 2 * xl)
    around = (seq + 2 - 4 * (seq // 2 % 2), ten + 1 - 2 * xl)
    beside = (seq + 1 - 2 * core, ten)
    ahead = (seq, (ten + 2) % (2 * Y))
    behind = (seq, (ten + 2 * Y - 2) % (2 * Y))
    neighbours = ((ahead, (seq, (ten + 3 - 2 * xl) % (2 * Y))), (behind, (seq, (ten + 2 * Y - 1 - 2 * xl) % (2 * Y))))
    width = factors.shape[2]
    columns = weight.shape[1]
    wide = columns // 2
    chunk = wide // CHUNKS
    half = CHUNKS // 2
    rows = BLOCK // Y
    group = S // GROUPS_OF_SLABS
    near = range(-group, 2 * group)

    inputs = [
        pltpu.make_async_copy(key_in, factors.at[0], i_sem.at[0]),
        pltpu.make_async_copy(value_in, factors.at[1], i_sem.at[0]),
        pltpu.make_async_copy(query_in, factors.at[2], i_sem.at[0]),
        pltpu.make_async_copy(filters_in, filters, i_sem.at[1]),
        pltpu.make_async_copy(skip_in, skip, i_sem.at[2]),
    ]
    for copy in inputs:
        copy.start()

    barrier = pltpu.get_barrier_semaphore()

    def greet(device):
        pl.semaphore_signal(barrier, inc=1, device_id=device, device_id_type=pl.DeviceIdType.MESH)

    for device in (across, around, *neighbours[0], *neighbours[1]):
        greet(device)

    def greet_seq(d, _):
        greet(((seq + d) % S, ten))
        return 0

    lax.fori_loop(1, S, greet_seq, 0, unroll=True)
    for k in near:
        if k != 0:
            greet(((seq + S + k) % S, ten + 1 - 2 * xl))

    def own_weight(j):
        return pltpu.make_async_copy(
            weight.at[:, pl.ds(pl.multiple_of(xl * wide + j * chunk, LANES), chunk)], wv.at[0, j], w_local.at[0]
        )

    for j in range(CHUNKS):
        own_weight(j).start()

    pltpu.make_async_copy(factors, factors, i_sem.at[0]).wait()
    inputs[3].wait()
    inputs[4].wait()

    def slabs(array):
        turned = array.T
        return jnp.concatenate(
            [turned[:, :LANES].reshape(S, SLAB, LANES), turned[:, LANES:].reshape(S, SLAB, LANES)], axis=1
        ).astype(BF16)

    sx[...] = slabs(factors[0].astype(F32) * factors[1].astype(F32))
    for g in range(filters.shape[0]):
        for h in range(2):
            sf[g, h : h + 1, :] = filters[g : g + 1, h * LANES : (h + 1) * LANES]
    rx[pl.ds(seq, 1)] = sx[pl.ds(seq, 1)]
    rf[pl.ds(seq, 1)] = sf[pl.ds(seq // 2, 1)]

    pl.semaphore_wait(barrier, S + 4 + 3 * group)

    def taps_copy(k):
        p = (seq + S - k) % S
        return remote(sf.at[p // 2], rf.at[seq], f_send.at[0], f_recv.at[0], (p, ten))

    def signal_copy(k):
        p = (seq + S - k) % S
        return remote(sx.at[p], rx.at[seq], x_send.at[0], x_recv.at[0], (p, ten))

    def response_copy(k):
        p = (seq + S - k) % S
        return remote(sg.at[p], rg.at[k], g_send.at[0], g_recv.at[k // group], (p, ten))

    def twin_copy(k):
        p = (seq + S - k) % S
        return remote(sg.at[p], hx.at[k + group], h_send.at[0], h_recv.at[0], (p, ten + 1 - 2 * xl))

    def relay(n):
        span = pl.ds(n * group, group)
        return remote(gk.at[span], gx.at[span], e_send.at[0], e_recv.at[n], across)

    middle = GROUPS_OF_SLABS // 2
    order = [middle]
    for n in range(1, middle):
        order += [middle - n, middle + n]
    order += [0]
    far = order[:-3]

    def each(function):
        function(S // 2)

        def step(m, _):
            function(S // 2 - m)
            function(S // 2 + m)
            return 0

        lax.fori_loop(1, S // 2, step, 0, unroll=True)

    each(lambda k: taps_copy(k).start())
    each(lambda k: signal_copy(k).start())
    sq[...] = slabs(factors[2].astype(F32))
    for k in near:
        remote(sq.at[(seq + S + k) % S], qx.at[k + group], h_send.at[1], h_recv.at[1], across).start()

    def direct(i):
        j = core * half + i
        return remote(
            weight.at[:, pl.ds(pl.multiple_of((1 - xl) * wide + j * chunk, LANES), chunk)],
            wv.at[1, j], wd_send.at[0], wd_recv.at[i], across if i % 2 == 0 else around,
        )

    def forward(i):
        j = core * half + i
        return remote(wv.at[1, j], wv.at[1, j], wf_send.at[0], wf_recv.at[i], beside)

    def forwarded(i):
        j = (1 - core) * half + i
        return remote(wv.at[1, j], wv.at[1, j], wf_send.at[0], wf_recv.at[i], beside)

    def direct_part(i, part_of):
        j = core * half + i
        span = pl.ds(part_of * (width // 2), width // 2)
        place = pl.ds(pl.multiple_of((1 - xl) * wide + j * chunk, LANES), chunk)
        return remote(
            weight.at[span, place], wv.at[1, j, span], wd_send.at[0], wd_recv.at[i], across if i % 2 == 0 else around
        )

    for i in range(half // 2):
        direct(i).start()
    for i in range(half // 2, half):
        direct_part(i, 0).start()

    everyone = pl.ds(0, S - 1)
    all_taps = remote(rf.at[everyone], rf.at[everyone], f_send.at[0], f_recv.at[0], across)
    all_signals = remote(rx.at[everyone], rx.at[everyone], x_send.at[0], x_recv.at[0], across)
    all_responses = remote(sg.at[everyone], rg.at[everyone], g_send.at[0], g_recv.at[0], across)
    relayed = pl.ds(2 * group, S - 3 * group)
    all_relays = remote(gk.at[relayed], gx.at[relayed], e_send.at[0], e_recv.at[0], across)
    all_twins = remote(hx, hx, h_send.at[0], h_recv.at[0], across)

    def some_responses(n):
        span = pl.ds(0, group if n > 0 else group - 1)
        return remote(sg.at[span], rg.at[span], g_send.at[0], g_recv.at[n], across)

    all_taps.wait_recv()
    toeplitz[0, 1, :, 0:LANES] = jnp.zeros((LANES, LANES), BF16)
    lane = lax.broadcasted_iota(jnp.int32, (LANES, LANES), 1)
    down = lax.broadcasted_iota(jnp.int32, (LANES, LANES), 0)
    mask = lane >= down

    def build(a, before):
        for h in range(2):
            row = jnp.broadcast_to(rf[a, h : h + 1, :], (LANES, LANES))
            rolled = pltpu.roll(row, 0, 1, stride=1, stride_axis=0)
            block = jnp.where(mask, rolled, before).astype(BF16)
            before = rolled
            if h == 0:
                toeplitz[a, 0, :, 0:LANES] = block
                toeplitz[a, 1, :, LANES:BLOCK] = block
            else:
                toeplitz[a, 0, :, LANES:BLOCK] = block
                toeplitz[a + 1, 1, :, 0:LANES] = block
        return before

    lax.fori_loop(0, S, build, jnp.zeros((LANES, LANES), F32), unroll=4)

    all_signals.wait_recv()
    signal = rx[...].astype(F32)
    for h in range(2):
        piece = signal[:, h * SLAB : (h + 1) * SLAB, :].reshape(S * SLAB, LANES)
        for r in range(UNROLL):
            shifted = piece
            if r > 0:
                shifted = jnp.concatenate([jnp.zeros((r * SLAB, LANES), F32), piece[: (S - r) * SLAB]], axis=0)
            lhs[:, r * BLOCK + h * LANES : r * BLOCK + (h + 1) * LANES] = shifted.astype(BF16)
    for step in range(S // UNROLL):
        top = step * UNROLL * SLAB
        taps = toeplitz[step * UNROLL : (step + 1) * UNROLL].reshape(UNROLL * BLOCK, BLOCK)
        product = jnp.dot(lhs[: S * SLAB - top, :], taps, preferred_element_type=F32)
        if step == 0:
            acc[...] = product
        else:
            acc[top:, :] += product
    spot = lax.broadcasted_iota(jnp.int32, (SLAB, width), 1) - SLAB * seq
    picked = spot == lax.broadcasted_iota(jnp.int32, (SLAB, width), 0)
    scale = jnp.sum(jnp.where(picked, skip[...], 0.0), axis=1, keepdims=True)
    pieces = []
    for h in range(2):
        response = acc[:, h * LANES : (h + 1) * LANES].reshape(S, SLAB, LANES)
        pieces.append(response + scale[None] * rx[...].astype(F32)[:, h * SLAB : (h + 1) * SLAB])
    sg[...] = jnp.concatenate(pieces, axis=1).astype(BF16)
    each(lambda k: response_copy(k).start())
    for k in reversed(near):
        twin_copy(k).start()
    for i in range(half // 2, half):
        direct_part(i, 1).start()
    rg[pl.ds(0, 1)] = sg[pl.ds(seq, 1)]

    pltpu.make_async_copy(wv.at[0], wv.at[0], w_local.at[0]).wait()

    def turn(side):
        for h in range(2):
            piece = gs[...].astype(F32)[:, h * SLAB : (h + 1) * SLAB].reshape(width, LANES)
            gated[side, h * LANES : (h + 1) * LANES, :] = piece.T.astype(BF16)

    for n in order:
        some_responses(n).wait_recv()
        for k in range(n * group, (n + 1) * group):
            s = (seq + k) % S
            slab = (sq[s].astype(F32) * rg[k].astype(F32)).astype(BF16)
            gk[k] = slab
            gs[s] = slab
        if n in far:
            relay(n).start()
    for i in range(half // 2):
        direct(i).wait_recv()
        forward(i).start()
    turn(0)

    def chunk_of(i, parity):
        return (core + parity) % 2 * half + i // 2

    for i in range(CHUNKS):
        term = jnp.dot(gated[0], wv[0, chunk_of(i, i % 2)], preferred_element_type=F32)
        part[i] = term.reshape(Y, 2, rows // 2, chunk)
    remote(qx, qx, h_send.at[1], h_recv.at[1], across).wait()
    all_twins.wait_recv()
    for k in near:
        gs[(seq + S + k) % S] = (qx[k + group].astype(F32) * hx[k + group].astype(F32)).astype(BF16)
    for n in far:
        relay(n).wait_recv()
    for k in range(2 * group, S - group):
        gs[(seq + k) % S] = gx[k]
    turn(1)

    steps = [((Y - 1) // 2, Y // 2), (Y // 2, (Y - 1) // 2)]

    def hop(i, slot, s, side):
        return remote(
            ss.at[i, slot], sr.at[i, s, side], r_send.at[0], r_recv.at[i, s], neighbours[side][0]
        )

    def last_hop(i, slot, side, apart):
        half_rows = ss.at[i, slot, (xl + apart) % 2]
        return remote(
            half_rows, lr.at[i, side, apart], r_send.at[0], l_recv.at[i], neighbours[side][apart]
        )

    def pairs(batch, function):
        def step(pair, _):
            for parity in range(2):
                function(2 * pair + parity, parity)
            return 0

        lax.fori_loop(batch * half // 2, (batch + 1) * half // 2, step, 0)

    def project(i, parity):
        j = chunk_of(i, parity)
        term = jnp.dot(gated[1], wv[1, j], preferred_element_type=F32)
        part[i] += term.reshape(Y, 2, rows // 2, chunk)
        fo[i] = part[i, y, 1 - xl].astype(BF16)
        remote(fo.at[i], fr.at[i], p_sem.at[0], p_sem.at[1], across).start()
        advance(0, i, parity)

    def advance(s, i, parity):
        up, low = steps[parity]
        if 0 < s < min(up, low):
            remote(sr.at[i, s - 1], sr.at[i, s - 1], r_send.at[0], r_recv.at[i, s - 1], ahead).wait_recv()
        elif 0 < s < max(up, low):
            hop(i, 0, s - 1, 0 if up > low else 1).wait_recv()
        for side, slot, count, owner in ((0, 0, up, (y + up - s) % Y), (1, up, low, (y + Y - low + s) % Y)):
            if s >= count:
                continue
            total = part[i, owner]
            if s > 0:
                total = total + sr[i, s - 1, side].astype(F32)
            ss[i, slot + s] = total.astype(BF16)
            if s < count - 1:
                hop(i, slot + s, s, side).start()
            else:
                last_hop(i, slot + s, side, 0).start()
                last_hop(i, slot + s, side, 1).start()

    def finish(i, parity):
        j = chunk_of(i, parity)
        remote(lr.at[i], lr.at[i], r_send.at[0], l_recv.at[i], ahead).wait_recv()
        for apart in range(2):
            total = part[i, y, xl] if apart == 0 else fr[i].astype(F32)
            for side in range(2):
                total = total + lr[i, side, apart].astype(F32)
            place = pl.ds(pl.multiple_of((xl + apart) % 2 * wide + j * chunk, LANES), chunk)
            out[:, place] = total.astype(BF16)

    for i in range(half):
        if i % 2 == 1:
            forwarded(i // 2).wait_recv()
        project(i, i % 2)
    all_taps.wait_send()
    all_signals.wait_send()
    all_responses.wait_send()
    all_relays.wait_send()
    all_twins.wait_send()
    for n in range(half // 2, half):
        direct(n).wait_recv()
        forward(n).start()
    last = Y // 2 - 1
    pairs(0, functools.partial(advance, 1))
    for i in range(half, CHUNKS):
        if i % 2 == 1:
            forwarded(i // 2).wait_recv()
        project(i, i % 2)
    for s in range(1, last):
        pairs(1, functools.partial(advance, s))
        if s + 1 < last:
            pairs(0, functools.partial(advance, s + 1))
    pairs(0, functools.partial(advance, last))
    remote(fo, fr, p_sem.at[0], p_sem.at[1], across).wait()
    pairs(1, functools.partial(advance, last))
    pairs(0, finish)
    pairs(1, finish)

    remote(wv.at[0, pl.ds(0, half)], wv.at[0, pl.ds(0, half)], wd_send.at[0], wd_recv.at[0], across).wait_send()
    remote(wv.at[1, pl.ds(0, half)], wv.at[1, pl.ds(0, half)], wf_send.at[0], wf_recv.at[0], beside).wait_send()
    remote(ss, ss, r_send.at[0], p_sem.at[1], ahead).wait_send()


def body(query, key_branch, value, filters, skip, weight):
    S = lax.axis_size("seq")
    T = lax.axis_size("tensor")
    Y = T // 2
    width = query.shape[1]
    columns = weight.shape[1]
    chunk = columns // 2 // CHUNKS
    rows = BLOCK // Y
    dma = pltpu.SemaphoreType.DMA
    slab = pltpu.VMEM((S, 2 * SLAB, LANES), BF16)
    return pl.pallas_call(
        functools.partial(kernel, S, Y),
        out_shape=pltpu.VMEM((BLOCK // T, columns), BF16),
        in_specs=[pl.BlockSpec(memory_space=pltpu.HBM)] * 6,
        out_specs=pl.BlockSpec(memory_space=pltpu.VMEM),
        scratch_shapes=[
            pltpu.VMEM((3, *query.shape), BF16), pltpu.VMEM(filters.shape, F32), pltpu.VMEM((1, width), F32), dma((3,)),
            slab, slab, slab,
            pltpu.VMEM((filters.shape[0], 2, LANES), F32), pltpu.VMEM((S, 2, LANES), F32),
            pltpu.VMEM((S + 1, 2, LANES, BLOCK), BF16),
            pltpu.VMEM((S * SLAB, UNROLL * BLOCK), BF16),
            pltpu.VMEM((S * SLAB, BLOCK), F32),
            slab, slab, slab, slab, slab,
            pltpu.VMEM((3 * S // GROUPS_OF_SLABS, 2 * SLAB, LANES), BF16),
            pltpu.VMEM((3 * S // GROUPS_OF_SLABS, 2 * SLAB, LANES), BF16),
            pltpu.VMEM((2, BLOCK, width), BF16),
            pltpu.VMEM((2, CHUNKS, width, chunk), BF16),
            pltpu.VMEM((CHUNKS, Y, 2, rows // 2, chunk), F32),
            pltpu.VMEM((CHUNKS, Y - 1, 2, rows // 2, chunk), BF16),
            pltpu.VMEM((CHUNKS, Y // 2 - 1, 2, 2, rows // 2, chunk), BF16),
            pltpu.VMEM((CHUNKS, 2, 2, rows // 2, chunk), BF16),
            pltpu.VMEM((CHUNKS, rows // 2, chunk), BF16),
            pltpu.VMEM((CHUNKS, rows // 2, chunk), BF16),
            dma((1,)), dma((1,)), dma((1,)), dma((1,)), dma((1,)), dma((GROUPS_OF_SLABS,)),
            dma((1,)), dma((GROUPS_OF_SLABS,)), dma((2,)), dma((2,)),
            dma((1,)),
            dma((1,)), dma((CHUNKS // 2,)), dma((1,)), dma((CHUNKS // 2,)),
            dma((1,)), dma((CHUNKS, Y // 2 - 1)), dma((CHUNKS,)), dma((2,)),
        ],
        compiler_params=pltpu.CompilerParams(
            collective_id=0, has_side_effects=True, vmem_limit_bytes=60 * 2**20
        ),
        name="hyena",
    )(query, key_branch, value, filters, skip.reshape(1, width), weight)


def solution(mesh):
    return jax.shard_map(
        body,
        mesh=mesh,
        in_specs=(
            P("seq", "tensor"),
            P("seq", "tensor"),
            P("seq", "tensor"),
            P("tensor", "seq"),
            P("tensor"),
            P("tensor", None),
        ),
        out_specs=P(("seq", "tensor"), None),
        check_vma=False,
    )
```
